1024 devices in a mesh: member: 8 (over z_hi, core), region: 128 (over z_lo, y, x).
Axes of the slice: x: 4, y: 4, z: 32 (z_hi: 4, z_lo: 8; z = z_hi * 8 + z_lo), core: 2. Of those that a mesh axis runs over, the one named last changes fastest.
Arguments:
- members: float32 [512, 8, 32768], P('member', None, 'region'), may hold values from -12 to 12
- weights: float32 [2, 512, 8, 32768], P(None, 'member', None, 'region'), may hold values from -6 to 6
- taper_table: float32 [8], replicated, may hold values from 0.1 to 1
- pair_blocks: int32 [1024, 2], P('region'), may hold values from 0 to 3, as said below
- pair_taper: int32 [1024], P('region'), may hold values from 0 to 7
- pair_batch: int32 [1024], P('region'), may hold values from 0 to 1
Outputs:
- analysis: float32 [512, 8, 32768], P('member', None, 'region')
The draws below stay inside these ranges and needn't reach their ends.
Inputs may be any that keep to these rules, and one draw needn't show every extreme that they name: `pair_blocks`: row p of group r is (t, s): t one of the region's 2 blocks and s = t + j with j in 0, 1, 2; no (t, s, pair_batch) repeats within a group; every group holds a pair with (t, s) = (0, 0) and one with (1, 3).
All inputs are finite; a program needn't handle non-finite values.
Results may differ from the reference program's by a relative error of at most 0.0003.
Values sent between devices are 32-bit elements; how exact they have to be, the bound alone decides.
No kernel may reach another device: no remote copies, remote signals or barrier semaphores. Data moves between devices by JAX's collectives and lax.ppermute only.
A program may use at most 32 MiB of HBM per device.

```python
import math
import jax
import jax.numpy as jnp
from jax import lax

M = 512
BLK = 128
NB_DEV = 2
NBATCH = 2
NTAPER = 8
L = 8
C = 32768
PAIR_DEV = 8
N_REGION = 128


def pair_lists(key):
    region_count = C // (NB_DEV * BLK)
    cand_count = 6 * NB_DEV

    def one_region(region_key):
        left_key, right_key, rank_key, order_key = jax.random.split(region_key, 4)
        left_pick = jax.random.randint(left_key, (), 0, 2, jnp.int32)
        right_pick = 6 * (NB_DEV - 1) + 4 + jax.random.randint(right_key, (), 0, 2, jnp.int32)
        rank_order = jax.random.permutation(rank_key, cand_count).astype(jnp.int32)
        labels = jnp.arange(cand_count, dtype=jnp.int32)
        rank_order = jnp.where(labels == left_pick, -2, jnp.where(labels == right_pick, -1, rank_order))
        chosen = jnp.argsort(rank_order, stable=True)[:PAIR_DEV].astype(jnp.int32)
        chosen = chosen[jax.random.permutation(order_key, PAIR_DEV)]
        target = chosen // 6
        source = target + chosen // 2 % 3
        return (jnp.stack([target, source], axis=-1).astype(jnp.int32), (chosen % 2).astype(jnp.int32))
    blocks, batches = jax.vmap(one_region)(jax.random.split(key, region_count))
    return (blocks.reshape(region_count * PAIR_DEV, 2), batches.reshape(region_count * PAIR_DEV))


def draw_pair_blocks(key, part):
    return pair_lists(key)[0]


def draw_pair_batch(key, part):
    return pair_lists(key)[1]


def draw_members(key, part):
    key = jax.random.fold_in(key, 11)
    center_key, spread_key, noise_key = jax.random.split(key, 3)
    center = 2.0 * jax.random.truncated_normal(center_key, -3.0, 3.0, (L, C), jnp.float32)
    spread = jnp.exp(jax.random.uniform(spread_key, (L, C), jnp.float32, math.log(0.5), math.log(1.5)))
    scatter_noise = jax.random.truncated_normal(noise_key, -4.0, 4.0, (M, L, C), jnp.float32)
    return center[None] + spread[None] * scatter_noise


def with_ends(values, own_key, least, top_value):
    extent = values.shape
    index_at = [jax.random.randint(jax.random.fold_in(own_key, axis), (), 0, extent[axis]) for axis in range(len(extent))]
    values = values.at[tuple(index_at)].set(least)
    longest = extent.index(max(extent))
    index_at[longest] = (index_at[longest] + 1) % extent[longest]
    return values.at[tuple(index_at)].set(top_value)


def block_scale(stream_key, shape, cuts, least, top_value):
    gain, own = 1.0, jax.random.fold_in(stream_key, 6)
    for axis_at, parts in cuts:
        steps = jnp.exp(jax.random.uniform(jax.random.fold_in(own, axis_at), (parts,), jnp.float32, least / len(cuts), top_value / len(cuts)))
        gain = gain * jnp.repeat(steps, shape[axis_at] // parts).reshape([-1 if axis == axis_at else 1 for axis in range(len(shape))])
    return gain


def centred(own_key, shape, deviation, bound, cuts=(), kind=jnp.bfloat16):
    loudness = block_scale(own_key, shape, cuts, -0.22, 0.18) if cuts else 1.0
    drawn = jax.random.normal(own_key, shape, jnp.float32) * deviation * loudness
    return jnp.minimum(jnp.maximum(drawn, -bound), bound).astype(kind)


def setup_inputs(seed: int = 0) -> dict:
    keys = jax.random.split(jax.random.key(seed), 7)
    return {
        "members": draw_members(jax.random.fold_in(keys[6], 71), 0),
        "weights": centred(keys[1], (NBATCH, M, L, C), 1.0, 6.0, ((1, 8), (3, 128)), jnp.float32),
        "taper_table": jnp.clip(jnp.exp(jax.random.uniform(keys[2], (NTAPER,), jnp.float32, math.log(0.1), math.log(1.0))), 0.1, 1.0),
        "pair_blocks": draw_pair_blocks(jax.random.fold_in(keys[6], 71), 0),
        "pair_taper": with_ends(jax.random.randint(keys[4], (PAIR_DEV * N_REGION,), 0, NTAPER), jax.random.fold_in(keys[4], 1), 0, NTAPER - 1).astype(jnp.int32),
        "pair_batch": draw_pair_batch(jax.random.fold_in(keys[6], 71), 0),
    }


def reference(members, weights, taper_table, pair_blocks, pair_taper, pair_batch):
    region_count = C // (NB_DEV * BLK)
    block_count = C // BLK
    member_mean = jnp.mean(members, axis=0)
    anomalies = members - member_mean[None]
    anom_blocks = anomalies.reshape(M, L, block_count, BLK)
    weight_blocks = weights.reshape(NBATCH, M, L, block_count, BLK)
    anom_padded = jnp.concatenate([anom_blocks[:, :, -1:], anom_blocks, anom_blocks[:, :, :1]], axis=2)
    weight_padded = jnp.concatenate([weight_blocks[:, :, :, -1:], weight_blocks, weight_blocks[:, :, :, :1]], axis=3)
    tapers = (taper_table[pair_taper] / (M - 1)).reshape(region_count, PAIR_DEV)
    blocks = pair_blocks.reshape(region_count, PAIR_DEV, 2)
    batches = pair_batch.reshape(region_count, PAIR_DEV)
    block_ids = jnp.arange(NB_DEV, dtype=jnp.int32)

    def one_region(region):
        first_block = (region * NB_DEV).astype(jnp.int32)
        anom_local = lax.dynamic_slice_in_dim(anom_padded, first_block, NB_DEV + 2, 2)
        weight_local = lax.dynamic_slice_in_dim(weight_padded, first_block, NB_DEV + 2, 3)

        def one_pair(accumulated, pair_index):
            target = blocks[region, pair_index, 0].astype(jnp.int32)
            source = blocks[region, pair_index, 1].astype(jnp.int32)
            target_anom = lax.dynamic_index_in_dim(anom_local, target + 1, 2, keepdims=False)
            source_anom = lax.dynamic_index_in_dim(anom_local, source, 2, keepdims=False)
            chosen = lax.dynamic_index_in_dim(weight_local, batches[region, pair_index].astype(jnp.int32), 0, keepdims=False)
            source_weight = lax.dynamic_index_in_dim(chosen, source, 2, keepdims=False)
            covariance = jnp.einsum('klc,kld->lcd', target_anom, source_anom, precision=lax.Precision.HIGHEST)
            pair_term = jnp.einsum('lcd,mld->mlc', covariance, source_weight, precision=lax.Precision.HIGHEST) * tapers[region, pair_index]
            placed = (block_ids == target).astype(jnp.float32)
            return accumulated + placed[None, None, :, None] * pair_term[:, :, None, :], None

        accumulated, _ = lax.scan(one_pair, jnp.zeros((M, L, NB_DEV, BLK), jnp.float32), jnp.arange(PAIR_DEV, dtype=jnp.int32))
        return accumulated

    pieces = lax.map(one_region, jnp.arange(region_count, dtype=jnp.int32))
    increment = jnp.transpose(pieces, (1, 2, 0, 3, 4)).reshape(M, L, C)
    return members + increment
```

```python
import functools

import jax
import jax.numpy as jnp
from jax import lax
from jax.experimental import pallas as pl
from jax.experimental.pallas import tpu as pltpu
from jax.sharding import PartitionSpec as P

BLK = 128
CHIPS = 4
GROUPS = [[2 * z + c for z in range(CHIPS)] for c in range(2)]
SWAP = [(i, i ^ 1) for i in range(2 * CHIPS)]
NEAR = [z ^ 1 for z in range(CHIPS)]
CROSS = [CHIPS - 1 - z for z in range(CHIPS)]


def pairing(step):
    moves = []
    for z in range(CHIPS):
        for core in range(2):
            partner = (NEAR if (core + step) % 2 == 0 else CROSS)[z]
            moves.append((2 * z + core, 2 * partner + core))
    return moves


def split(x):
    high = x.astype(jnp.bfloat16)
    return high, (x - high.astype(jnp.float32)).astype(jnp.bfloat16)


def product(a, b, dims):
    (ah, al), (bh, bl) = a, b
    dot = functools.partial(
        lax.dot_general, dimension_numbers=(dims, ((), ())), preferred_element_type=jnp.float32
    )
    return dot(ah, bh) + (dot(ah, bl) + dot(al, bh))


ROWS = ((0,), (0,))
PLAIN = ((1,), (0,))
LANES = ((1,), (1,))


def anomaly_kernel(a_ref, b_ref, c_ref, out_ref):
    a, b, c = a_ref[...], b_ref[...], c_ref[...]
    count = a.shape[0] + b.shape[0] + c.shape[0]
    total = (
        jnp.sum(a, axis=0, keepdims=True)
        + jnp.sum(b, axis=0, keepdims=True)
        + jnp.sum(c, axis=0, keepdims=True)
    )
    mean = total / count
    out_ref[: a.shape[0]] = a - mean
    out_ref[a.shape[0] : a.shape[0] + b.shape[0]] = b - mean
    out_ref[a.shape[0] + b.shape[0] :] = c - mean


def anomalies_of(parts):
    count = sum(p.shape[0] for p in parts)
    return pl.pallas_call(
        anomaly_kernel, out_shape=jax.ShapeDtypeStruct((count, BLK), jnp.float32)
    )(*parts)


def covariance_kernel(first_ref, second_ref, after_ref, edge_ref, own_ref):
    first, second, after = (split(r[...]) for r in (first_ref, second_ref, after_ref))
    edge_ref[...] = product(second, after, ROWS)
    d0 = product(first, first, ROWS)
    d1 = product(second, second, ROWS)
    row = lax.broadcasted_iota(jnp.int32, (BLK, BLK), 0)
    col = lax.broadcasted_iota(jnp.int32, (BLK, BLK), 1)
    own_ref[:BLK] = jnp.where(row <= col, d0, d1)
    own_ref[BLK : 2 * BLK] = product(first, second, ROWS)
    diagonal = jnp.sum(jnp.where(row == col, d1, 0.0), axis=0, keepdims=True)
    own_ref[2 * BLK :] = jnp.broadcast_to(diagonal, (8, BLK))


def covariances(first, second, after):
    return pl.pallas_call(
        covariance_kernel,
        out_shape=(
            jax.ShapeDtypeStruct((BLK, BLK), jnp.float32),
            jax.ShapeDtypeStruct((2 * BLK + 8, BLK), jnp.float32),
        ),
    )(first, second, after)


def increment_kernel(coef_ref, w_ref, wl_ref, wr_ref, own_ref, edge_ref, left_ref, out_ref):
    row = lax.broadcasted_iota(jnp.int32, (BLK, BLK), 0)
    col = lax.broadcasted_iota(jnp.int32, (BLK, BLK), 1)
    packed = own_ref[0, :BLK]
    upper = jnp.where(row <= col, packed, 0.0)
    strict = jnp.where(row < col, packed, 0.0)
    lower = jnp.where(row > col, packed, 0.0)
    d0 = split(upper + strict.T)
    d1 = split(lower + lower.T + jnp.where(row == col, own_ref[0, 2 * BLK : 2 * BLK + 1], 0.0))
    c01 = split(own_ref[0, BLK : 2 * BLK])
    edge = split(edge_ref[0])
    left = split(left_ref[0])

    def mixed(t, j, block):
        at = t * 6 + j * 2
        part = pl.ds(block * BLK, BLK)
        return split(coef_ref[at] * w_ref[0, 0, :, part] + coef_ref[at + 1] * w_ref[1, 0, :, part])

    out_ref[0, :, :BLK] = (
        product(split(wl_ref[0]), left, PLAIN)
        + product(mixed(0, 1, 0), d0, PLAIN)
        + product(mixed(0, 2, 1), c01, LANES)
    )
    out_ref[0, :, BLK:] = (
        product(mixed(1, 0, 0), c01, PLAIN)
        + product(mixed(1, 1, 1), d1, PLAIN)
        + product(split(wr_ref[0]), edge, LANES)
    )


def increments(coefs, w, w_left, w_right, own, edge, left):
    levels, members = w.shape[1:3]
    per_level = lambda *shape: pl.BlockSpec((1,) + shape, lambda i: (i, 0, 0))
    return pl.pallas_call(
        increment_kernel,
        grid=(levels,),
        in_specs=[
            pl.BlockSpec(memory_space=pltpu.SMEM),
            pl.BlockSpec((2, 1, members, 2 * BLK), lambda i: (0, i, 0, 0)),
            per_level(members, BLK),
            per_level(members, BLK),
            per_level(2 * BLK + 8, BLK),
            per_level(BLK, BLK),
            per_level(BLK, BLK),
        ],
        out_specs=per_level(members, 2 * BLK),
        out_shape=jax.ShapeDtypeStruct((levels, members, 2 * BLK), jnp.float32),
    )(coefs, w, w_left, w_right, own, edge, left)


def one_hot(index, count):
    return (index[:, None] == jnp.arange(count, dtype=jnp.int32)[None, :]).astype(jnp.float32)


def pick(x, index):
    return lax.dynamic_index_in_dim(x, index, 0, keepdims=False)


def local(members, weights, taper_table, pair_blocks, pair_taper, pair_batch):
    member_loc, levels, _ = members.shape
    ensemble = member_loc * lax.axis_size("member")
    regions = lax.axis_size("region")
    right = [(i, (i + 1) % regions) for i in range(regions)]
    left = [(j, i) for i, j in right]
    me = lax.axis_index("member")
    chip, core = me // 2, me % 2
    half = levels // 2

    states = jnp.transpose(members, (1, 0, 2))
    mine = lax.dynamic_slice_in_dim(states, core * half, half, 0)
    theirs = lax.dynamic_slice_in_dim(states, (1 - core) * half, half, 0)
    states = jnp.concatenate([mine, lax.ppermute(theirs, "member", SWAP)], axis=1)

    near = chip ^ 1
    cross = CHIPS - 1 - chip
    one = jnp.where(core == 0, near, cross)
    two = jnp.where(core == 0, cross, near)
    both = CHIPS - 1 - near
    step_one, step_two = pairing(0), pairing(1)

    def to_owner(block):
        x = states[:, :, block * BLK : (block + 1) * BLK]
        got = lax.ppermute(jnp.stack([pick(x, one), pick(x, both)]), "member", step_one)
        last = lax.ppermute(jnp.stack([pick(x, two), got[1]]), "member", step_two)
        return anomalies_of([pick(x, chip), got[0], last.reshape(-1, BLK)])

    first = to_owner(0)
    second = to_owner(1)
    after = lax.ppermute(first, "region", left)

    tapers = jnp.dot(
        one_hot(pair_taper, taper_table.shape[0]), taper_table, precision=lax.Precision.HIGHEST
    ) / (ensemble - 1)
    targets = pair_blocks[:, 0]
    slot = targets * 6 + (pair_blocks[:, 1] - targets) * 2 + pair_batch
    coefs = jnp.sum(one_hot(slot, 12) * tapers[:, None], axis=0)
    from_right = lax.ppermute(coefs, "region", left)
    from_left = lax.ppermute(coefs, "region", right)

    w = jnp.transpose(weights, (0, 2, 1, 3))
    mine = lax.dynamic_slice_in_dim(w, core * half, half, 1)
    theirs = lax.dynamic_slice_in_dim(w, (1 - core) * half, half, 1)
    w = jnp.concatenate([mine, lax.ppermute(theirs, "member", SWAP)], axis=2)
    w_first, w_last = w[..., :BLK], w[..., BLK:]
    w_left = lax.ppermute(
        from_right[0] * w_last[0] + from_right[1] * w_last[1], "region", right
    )
    w_right = lax.ppermute(
        from_left[10] * w_first[0] + from_left[11] * w_first[1], "region", left
    )

    edge, own = covariances(first, second, after)
    edges = lax.all_gather(edge, "member", axis_index_groups=GROUPS)
    left_edges = lax.ppermute(edges, "region", right)
    owns = lax.all_gather(own, "member", axis_index_groups=GROUPS)

    change = increments(coefs, w, w_left, w_right, owns, edges, left_edges)
    kept = change[:, :member_loc]
    came = lax.ppermute(change[:, member_loc:], "member", SWAP)
    change = jnp.where(
        core == 0, jnp.concatenate([kept, came]), jnp.concatenate([came, kept])
    )
    return members + jnp.transpose(change, (1, 0, 2))


def solution(mesh):
    placed = (
        P("member", None, "region"),
        P(None, "member", None, "region"),
        P(),
        P("region", None),
        P("region"),
        P("region"),
    )
    return jax.shard_map(
        local, mesh=mesh, in_specs=placed, out_specs=P("member", None, "region"), check_vma=False
    )
```

```python
import functools

import jax
import jax.numpy as jnp
from jax import lax
from jax.experimental import pallas as pl
from jax.experimental.pallas import tpu as pltpu
from jax.sharding import PartitionSpec as P

BLK = 128
CHIPS = 4
GROUPS = [[2 * z + c for z in range(CHIPS)] for c in range(2)]
SWAP = [(i, i ^ 1) for i in range(2 * CHIPS)]
NEAR = [z ^ 1 for z in range(CHIPS)]
CROSS = [CHIPS - 1 - z for z in range(CHIPS)]


def pairing(step):
    moves = []
    for z in range(CHIPS):
        for core in range(2):
            partner = (NEAR if (core + step) % 2 == 0 else CROSS)[z]
            moves.append((2 * z + core, 2 * partner + core))
    return moves


def split(x):
    high = x.astype(jnp.bfloat16)
    return high, (x - high.astype(jnp.float32)).astype(jnp.bfloat16)


def product(a, b, dims):
    (ah, al), (bh, bl) = a, b
    dot = functools.partial(
        lax.dot_general, dimension_numbers=(dims, ((), ())), preferred_element_type=jnp.float32
    )
    return dot(ah, bh) + (dot(ah, bl) + dot(al, bh))


ROWS = ((0,), (0,))
PLAIN = ((1,), (0,))
LANES = ((1,), (1,))


def covariance_kernel(first_ref, kept_ref, got_ref, last_ref, after_ref, edge_ref, own_ref):
    def centred(*parts):
        count = sum(p.shape[0] for p in parts)
        mean = sum(jnp.sum(p, axis=0, keepdims=True) for p in parts) / count
        return split(jnp.concatenate([p - mean for p in parts], axis=0))

    second = centred(kept_ref[...], got_ref[...], last_ref[...])
    after = centred(after_ref[...])
    edge_ref[...] = product(second, after, ROWS)
    first = centred(first_ref[...])
    d0 = product(first, first, ROWS)
    d1 = product(second, second, ROWS)
    row = lax.broadcasted_iota(jnp.int32, (BLK, BLK), 0)
    col = lax.broadcasted_iota(jnp.int32, (BLK, BLK), 1)
    own_ref[:BLK] = jnp.where(row <= col, d0, d1)
    own_ref[BLK : 2 * BLK] = product(first, second, ROWS)
    diagonal = jnp.sum(jnp.where(row == col, d1, 0.0), axis=0, keepdims=True)
    own_ref[2 * BLK :] = jnp.broadcast_to(diagonal, (8, BLK))


LONG = pl.CostEstimate(flops=50_000_000_000, bytes_accessed=200_000_000, transcendentals=0)
TINY = pl.CostEstimate(flops=1000, bytes_accessed=1000, transcendentals=0)


def covariances(*parts):
    return pl.pallas_call(
        covariance_kernel,
        out_shape=(
            jax.ShapeDtypeStruct((BLK, BLK), jnp.float32),
            jax.ShapeDtypeStruct((2 * BLK + 8, BLK), jnp.float32),
        ),
        cost_estimate=TINY,
    )(*parts)


def increment_kernel(coef_ref, w_ref, wl_ref, wr_ref, own_ref, edge_ref, left_ref, kept_ref, sent_ref):
    row = lax.broadcasted_iota(jnp.int32, (BLK, BLK), 0)
    col = lax.broadcasted_iota(jnp.int32, (BLK, BLK), 1)
    packed = own_ref[0, :BLK]
    upper = jnp.where(row <= col, packed, 0.0)
    strict = jnp.where(row < col, packed, 0.0)
    lower = jnp.where(row > col, packed, 0.0)
    d0 = split(upper + strict.T)
    d1 = split(lower + lower.T + jnp.where(row == col, own_ref[0, 2 * BLK : 2 * BLK + 1], 0.0))
    c01 = split(own_ref[0, BLK : 2 * BLK])
    edge = split(edge_ref[0])
    left = split(left_ref[0])

    def mixed(ref, t, j, part=slice(None)):
        at = t * 6 + j * 2
        return split(coef_ref[at] * ref[0, 0, :, part] + coef_ref[at + 1] * ref[1, 0, :, part])

    here, there = slice(0, BLK), slice(BLK, 2 * BLK)
    zero = (
        product(mixed(wl_ref, 0, 0), left, PLAIN)
        + product(mixed(w_ref, 0, 1, here), d0, PLAIN)
        + product(mixed(w_ref, 0, 2, there), c01, LANES)
    )
    one = (
        product(mixed(w_ref, 1, 0, here), c01, PLAIN)
        + product(mixed(w_ref, 1, 1, there), d1, PLAIN)
        + product(mixed(wr_ref, 1, 2), edge, LANES)
    )
    keep = kept_ref.shape[1]
    for ref, rows in ((kept_ref, slice(0, keep)), (sent_ref, slice(keep, 2 * keep))):
        ref[0, :, here] = zero[rows]
        ref[0, :, there] = one[rows]


def increments(coefs, w, w_left, w_right, own, edge, left):
    levels, members = w.shape[1:3]
    per_level = lambda *shape: pl.BlockSpec((1,) + shape, lambda i: (i, 0, 0))
    both = lambda width: pl.BlockSpec((2, 1, members, width), lambda i: (0, i, 0, 0))
    half = jax.ShapeDtypeStruct((levels, members // 2, 2 * BLK), jnp.float32)
    return pl.pallas_call(
        increment_kernel,
        grid=(levels,),
        in_specs=[
            pl.BlockSpec(memory_space=pltpu.SMEM),
            both(2 * BLK),
            both(BLK),
            both(BLK),
            per_level(2 * BLK + 8, BLK),
            per_level(BLK, BLK),
            per_level(BLK, BLK),
        ],
        out_specs=(per_level(members // 2, 2 * BLK),) * 2,
        out_shape=(half, half),
        cost_estimate=TINY,
    )(coefs, w, w_left, w_right, own, edge, left)


def gather_kernel(mine_ref, got_ref, w_ref, low_ref, high_ref):
    keep = mine_ref.shape[2]
    for ref, rows in ((mine_ref, slice(0, keep)), (got_ref, slice(keep, 2 * keep))):
        w_ref[0, :, rows] = ref[0]
        low_ref[0, :, rows] = ref[0, :, :, :BLK]
        high_ref[0, :, rows] = ref[0, :, :, BLK:]


def gathered(mine, got):
    batches, levels, members, width = mine.shape
    block = lambda m, c: pl.BlockSpec((1, levels, m, c), lambda i: (i, 0, 0, 0))
    shape = lambda c: jax.ShapeDtypeStruct((batches, levels, 2 * members, c), jnp.float32)
    return pl.pallas_call(
        gather_kernel,
        grid=(batches,),
        in_specs=[block(members, width)] * 2,
        out_specs=(block(2 * members, width),) + (block(2 * members, BLK),) * 2,
        out_shape=(shape(width), shape(BLK), shape(BLK)),
        cost_estimate=LONG,
    )(mine, got)


def one_hot(index, count):
    return (index[:, None] == jnp.arange(count, dtype=jnp.int32)[None, :]).astype(jnp.float32)


def pick(x, index):
    return lax.dynamic_index_in_dim(x, index, 0, keepdims=False)


def local(members, weights, taper_table, pair_blocks, pair_taper, pair_batch):
    member_loc, levels, _ = members.shape
    ensemble = member_loc * lax.axis_size("member")
    regions = lax.axis_size("region")
    right = [(i, (i + 1) % regions) for i in range(regions)]
    left = [(j, i) for i, j in right]
    me = lax.axis_index("member")
    chip, core = me // 2, me % 2
    half = levels // 2

    states = jnp.transpose(members, (1, 0, 2))
    mine = lax.dynamic_slice_in_dim(states, core * half, half, 0)
    theirs = lax.dynamic_slice_in_dim(states, (1 - core) * half, half, 0)
    theirs, weights = lax.optimization_barrier((theirs, weights))
    states = jnp.concatenate([mine, lax.ppermute(theirs, "member", SWAP)], axis=1)

    near = chip ^ 1
    cross = CHIPS - 1 - chip
    one = jnp.where(core == 0, near, cross)
    two = jnp.where(core == 0, cross, near)
    both = CHIPS - 1 - near
    step_one, step_two = pairing(0), pairing(1)

    def to_owner(block):
        x = states[:, :, block * BLK : (block + 1) * BLK]
        got = lax.ppermute(jnp.stack([pick(x, one), pick(x, both)]), "member", step_one)
        last = lax.ppermute(jnp.stack([pick(x, two), got[1]]), "member", step_two)
        return pick(x, chip), got[0], last.reshape(-1, BLK)

    first = jnp.concatenate(to_owner(0))
    second = to_owner(1)
    after = lax.ppermute(first, "region", left)

    tapers = jnp.dot(
        one_hot(pair_taper, taper_table.shape[0]), taper_table, precision=lax.Precision.HIGHEST
    ) / (ensemble - 1)
    targets = pair_blocks[:, 0]
    slot = targets * 6 + (pair_blocks[:, 1] - targets) * 2 + pair_batch
    coefs = jnp.sum(one_hot(slot, 12) * tapers[:, None], axis=0)

    w = jnp.transpose(weights, (0, 2, 1, 3))
    mine = lax.dynamic_slice_in_dim(w, core * half, half, 1)
    theirs = lax.dynamic_slice_in_dim(w, (1 - core) * half, half, 1)
    w, low, high = gathered(mine, lax.ppermute(theirs, "member", SWAP))
    w_left = lax.ppermute(high, "region", right)
    w_right = lax.ppermute(low, "region", left)

    edge, own = covariances(first, *second, after)
    edges = lax.all_gather(edge, "member", axis_index_groups=GROUPS)
    left_edges = lax.ppermute(edges, "region", right)
    owns = lax.all_gather(own, "member", axis_index_groups=GROUPS)

    kept, sent = increments(coefs, w, w_left, w_right, owns, edges, left_edges)
    came = lax.ppermute(sent, "member", SWAP)
    change = jnp.where(
        core == 0, jnp.concatenate([kept, came]), jnp.concatenate([came, kept])
    )
    return members + jnp.transpose(change, (1, 0, 2))


def solution(mesh):
    placed = (
        P("member", None, "region"),
        P(None, "member", None, "region"),
        P(),
        P("region", None),
        P("region"),
        P("region"),
    )
    return jax.shard_map(
        local, mesh=mesh, in_specs=placed, out_specs=P("member", None, "region"), check_vma=False
    )
```

```python
import functools

import jax
import jax.numpy as jnp
from jax import lax
from jax.experimental import pallas as pl
from jax.experimental.pallas import tpu as pltpu
from jax.sharding import PartitionSpec as P

BLK = 128
CHIPS = 4
GROUPS = [[2 * z + c for z in range(CHIPS)] for c in range(2)]
SWAP = [(i, i ^ 1) for i in range(2 * CHIPS)]
NEAR = [z ^ 1 for z in range(CHIPS)]
CROSS = [CHIPS - 1 - z for z in range(CHIPS)]


def pairing(step):
    moves = []
    for z in range(CHIPS):
        for core in range(2):
            partner = (NEAR if (core + step) % 2 == 0 else CROSS)[z]
            moves.append((2 * z + core, 2 * partner + core))
    return moves


def split(x):
    high = x.astype(jnp.bfloat16)
    return high, (x - high.astype(jnp.float32)).astype(jnp.bfloat16)


def product(a, b, dims):
    (ah, al), (bh, bl) = a, b
    dot = functools.partial(
        lax.dot_general, dimension_numbers=(dims, ((), ())), preferred_element_type=jnp.float32
    )
    return dot(ah, bh) + (dot(ah, bl) + dot(al, bh))


ROWS = ((0,), (0,))
PLAIN = ((1,), (0,))
LANES = ((1,), (1,))


def centred(*parts):
    count = sum(p.shape[0] for p in parts)
    mean = sum(jnp.sum(p, axis=0, keepdims=True) for p in parts) / count
    return split(jnp.concatenate([p - mean for p in parts], axis=0))


def first_kernel(message_ref, high_ref, low_ref, square_ref):
    first = centred(message_ref[: high_ref.shape[0]])
    high_ref[...], low_ref[...] = first
    square_ref[...] = product(first, first, ROWS)


def covariance_kernel(
    high_ref, low_ref, square_ref, kept_ref, got_ref, last_ref, message_ref, edge_ref, own_ref
):
    second = centred(kept_ref[...], got_ref[...], last_ref[...])
    after = centred(message_ref[: high_ref.shape[0]])
    edge_ref[...] = product(second, after, ROWS)
    first = high_ref[...], low_ref[...]
    d1 = product(second, second, ROWS)
    row = lax.broadcasted_iota(jnp.int32, (BLK, BLK), 0)
    col = lax.broadcasted_iota(jnp.int32, (BLK, BLK), 1)
    own_ref[:BLK] = jnp.where(row <= col, square_ref[...], d1)
    own_ref[BLK : 2 * BLK] = product(first, second, ROWS)
    diagonal = jnp.sum(jnp.where(row == col, d1, 0.0), axis=0, keepdims=True)
    own_ref[2 * BLK :] = jnp.broadcast_to(diagonal, (8, BLK))


LONG = pl.CostEstimate(flops=50_000_000_000, bytes_accessed=200_000_000, transcendentals=0)
TINY = pl.CostEstimate(flops=1000, bytes_accessed=1000, transcendentals=0)


def covariances(message, kept, got, last, after):
    ensemble = message.shape[0] - 8
    square = jax.ShapeDtypeStruct((BLK, BLK), jnp.float32)
    half = jax.ShapeDtypeStruct((ensemble, BLK), jnp.bfloat16)
    first = pl.pallas_call(first_kernel, out_shape=(half, half, square), cost_estimate=LONG)(message)
    return pl.pallas_call(
        covariance_kernel,
        out_shape=(square, jax.ShapeDtypeStruct((2 * BLK + 8, BLK), jnp.float32)),
        cost_estimate=TINY,
    )(*first, kept, got, last, after)


def outward_kernel(message_ref, w_ref, edge_ref, out_ref):
    mixed = message_ref[:1, :1] * w_ref[0, 0] + message_ref[:1, 1:2] * w_ref[1, 0]
    out_ref[0] = product(split(mixed), split(edge_ref[0]), PLAIN)


def outward(message, w, edge):
    levels, members = w.shape[1:3]
    per_level = pl.BlockSpec((1, BLK, BLK), lambda i: (i, 0, 0))
    return pl.pallas_call(
        outward_kernel,
        grid=(levels,),
        in_specs=[
            pl.BlockSpec((8, BLK), lambda i: (message.shape[0] // 8 - 1, 0)),
            pl.BlockSpec((2, 1, members, BLK), lambda i: (0, i, 0, 1)),
            per_level,
        ],
        out_specs=per_level,
        out_shape=jax.ShapeDtypeStruct((levels, members, BLK), jnp.float32),
        cost_estimate=TINY,
    )(message, w, edge)


def increment_kernel(coef_ref, w_ref, wr_ref, own_ref, edge_ref, left_ref, kept_ref, sent_ref):
    row = lax.broadcasted_iota(jnp.int32, (BLK, BLK), 0)
    col = lax.broadcasted_iota(jnp.int32, (BLK, BLK), 1)
    packed = own_ref[0, :BLK]
    upper = jnp.where(row <= col, packed, 0.0)
    strict = jnp.where(row < col, packed, 0.0)
    lower = jnp.where(row > col, packed, 0.0)
    d0 = split(upper + strict.T)
    d1 = split(lower + lower.T + jnp.where(row == col, own_ref[0, 2 * BLK : 2 * BLK + 1], 0.0))
    c01 = split(own_ref[0, BLK : 2 * BLK])
    edge = split(edge_ref[0])

    def mixed(ref, t, j, part=slice(None)):
        at = t * 6 + j * 2
        return split(coef_ref[at] * ref[0, 0, :, part] + coef_ref[at + 1] * ref[1, 0, :, part])

    here, there = slice(0, BLK), slice(BLK, 2 * BLK)
    zero = (
        left_ref[0]
        + product(mixed(w_ref, 0, 1, here), d0, PLAIN)
        + product(mixed(w_ref, 0, 2, there), c01, LANES)
    )
    one = (
        product(mixed(w_ref, 1, 0, here), c01, PLAIN)
        + product(mixed(w_ref, 1, 1, there), d1, PLAIN)
        + product(mixed(wr_ref, 1, 2), edge, LANES)
    )
    keep = kept_ref.shape[1]
    for ref, rows in ((kept_ref, slice(0, keep)), (sent_ref, slice(keep, 2 * keep))):
        ref[0, :, here] = zero[rows]
        ref[0, :, there] = one[rows]


def increments(coefs, w, w_right, own, edge, left):
    levels, members = w.shape[1:3]
    per_level = lambda *shape: pl.BlockSpec((1,) + shape, lambda i: (i, 0, 0))
    both = lambda width: pl.BlockSpec((2, 1, members, width), lambda i: (0, i, 0, 0))
    half = jax.ShapeDtypeStruct((levels, members // 2, 2 * BLK), jnp.float32)
    return pl.pallas_call(
        increment_kernel,
        grid=(levels,),
        in_specs=[
            pl.BlockSpec(memory_space=pltpu.SMEM),
            both(2 * BLK),
            both(BLK),
            per_level(2 * BLK + 8, BLK),
            per_level(BLK, BLK),
            per_level(members, BLK),
        ],
        out_specs=(per_level(members // 2, 2 * BLK),) * 2,
        out_shape=(half, half),
        cost_estimate=TINY,
    )(coefs, w, w_right, own, edge, left)


def gather_kernel(mine_ref, got_ref, w_ref, low_ref):
    keep = mine_ref.shape[2]
    for ref, rows in ((mine_ref, slice(0, keep)), (got_ref, slice(keep, 2 * keep))):
        w_ref[0, :, rows] = ref[0]
        low_ref[0, :, rows] = ref[0, :, :, :BLK]


def gathered(mine, got):
    batches, levels, members, width = mine.shape
    block = lambda m, c: pl.BlockSpec((1, levels, m, c), lambda i: (i, 0, 0, 0))
    shape = lambda c: jax.ShapeDtypeStruct((batches, levels, 2 * members, c), jnp.float32)
    return pl.pallas_call(
        gather_kernel,
        grid=(batches,),
        in_specs=[block(members, width)] * 2,
        out_specs=(block(2 * members, width), block(2 * members, BLK)),
        out_shape=(shape(width), shape(BLK)),
        cost_estimate=LONG,
    )(mine, got)


def one_hot(index, count):
    return (index[:, None] == jnp.arange(count, dtype=jnp.int32)[None, :]).astype(jnp.float32)


def pick(x, index):
    return lax.dynamic_index_in_dim(x, index, 0, keepdims=False)


def local(members, weights, taper_table, pair_blocks, pair_taper, pair_batch):
    member_loc, levels, _ = members.shape
    ensemble = member_loc * lax.axis_size("member")
    regions = lax.axis_size("region")
    right = [(i, (i + 1) % regions) for i in range(regions)]
    left = [(j, i) for i, j in right]
    me = lax.axis_index("member")
    chip, core = me // 2, me % 2
    half = levels // 2

    states = jnp.transpose(members, (1, 0, 2))
    mine = lax.dynamic_slice_in_dim(states, core * half, half, 0)
    theirs = lax.dynamic_slice_in_dim(states, (1 - core) * half, half, 0)
    theirs, weights = lax.optimization_barrier((theirs, weights))
    states = jnp.concatenate([mine, lax.ppermute(theirs, "member", SWAP)], axis=1)

    near = chip ^ 1
    cross = CHIPS - 1 - chip
    one = jnp.where(core == 0, near, cross)
    two = jnp.where(core == 0, cross, near)
    both = CHIPS - 1 - near
    step_one, step_two = pairing(0), pairing(1)

    def to_owner(block):
        x = states[:, :, block * BLK : (block + 1) * BLK]
        got = lax.ppermute(jnp.stack([pick(x, one), pick(x, both)]), "member", step_one)
        last = lax.ppermute(jnp.stack([pick(x, two), got[1]]), "member", step_two)
        return pick(x, chip), got[0], last.reshape(-1, BLK)

    first, second = to_owner(0), to_owner(1)
    taken, pair_taper = lax.optimization_barrier((second[1], pair_taper))
    second = second[0], taken, second[2]
    tapers = jnp.dot(
        one_hot(pair_taper, taper_table.shape[0]), taper_table, precision=lax.Precision.HIGHEST
    ) / (ensemble - 1)
    targets = pair_blocks[:, 0]
    slot = targets * 6 + (pair_blocks[:, 1] - targets) * 2 + pair_batch
    coefs = jnp.sum(one_hot(slot, 12) * tapers[:, None], axis=0)
    rows = jnp.pad(coefs[None], ((0, 7), (0, BLK - 12)))
    message = jnp.concatenate([*first, rows])
    after = lax.ppermute(message, "region", left)

    w = jnp.transpose(weights, (0, 2, 1, 3))
    mine = lax.dynamic_slice_in_dim(w, core * half, half, 1)
    theirs = lax.dynamic_slice_in_dim(w, (1 - core) * half, half, 1)
    w, low = gathered(mine, lax.ppermute(theirs, "member", SWAP))
    w_right = lax.ppermute(low, "region", left)

    edge, own = covariances(message, *second, after)
    edges = lax.all_gather(edge, "member", axis_index_groups=GROUPS)
    from_left = lax.ppermute(outward(after, w, edges), "region", right)
    owns = lax.all_gather(own, "member", axis_index_groups=GROUPS)

    kept, sent = increments(coefs, w, w_right, owns, edges, from_left)
    came = lax.ppermute(sent, "member", SWAP)
    change = jnp.where(
        core == 0, jnp.concatenate([kept, came]), jnp.concatenate([came, kept])
    )
    return members + jnp.transpose(change, (1, 0, 2))


def solution(mesh):
    placed = (
        P("member", None, "region"),
        P(None, "member", None, "region"),
        P(),
        P("region", None),
        P("region"),
        P("region"),
    )
    return jax.shard_map(
        local, mesh=mesh, in_specs=placed, out_specs=P("member", None, "region"), check_vma=False
    )
```

```python
import functools

import jax
import jax.numpy as jnp
from jax import lax
from jax.experimental import pallas as pl
from jax.experimental.pallas import tpu as pltpu
from jax.sharding import PartitionSpec as P

BLK = 128
CHIPS = 4
GROUPS = [[2 * z + c for z in range(CHIPS)] for c in range(2)]
SWAP = [(i, i ^ 1) for i in range(2 * CHIPS)]
NEAR = [z ^ 1 for z in range(CHIPS)]
CROSS = [CHIPS - 1 - z for z in range(CHIPS)]


def pairing(step):
    moves = []
    for z in range(CHIPS):
        for core in range(2):
            partner = (NEAR if (core + step) % 2 == 0 else CROSS)[z]
            moves.append((2 * z + core, 2 * partner + core))
    return moves


def split(x):
    high = x.astype(jnp.bfloat16)
    return high, (x - high.astype(jnp.float32)).astype(jnp.bfloat16)


def product(a, b, dims):
    (ah, al), (bh, bl) = a, b
    dot = functools.partial(
        lax.dot_general, dimension_numbers=(dims, ((), ())), preferred_element_type=jnp.float32
    )
    return dot(ah, bh) + (dot(ah, bl) + dot(al, bh))


ROWS = ((0,), (0,))
PLAIN = ((1,), (0,))
LANES = ((1,), (1,))


def centred(*parts):
    count = sum(p.shape[0] for p in parts)
    mean = sum(jnp.sum(p, axis=0, keepdims=True) for p in parts) / count
    return split(jnp.concatenate([p - mean for p in parts], axis=0))


def first_kernel(message_ref, high_ref, low_ref, square_ref):
    first = centred(message_ref[: high_ref.shape[0]])
    high_ref[...], low_ref[...] = first
    square_ref[...] = product(first, first, ROWS)


def covariance_kernel(
    high_ref, low_ref, square_ref, kept_ref, got_ref, last_ref, message_ref, out_ref
):
    second = centred(kept_ref[...], got_ref[...], last_ref[...])
    first = high_ref[...], low_ref[...]
    d1 = product(second, second, ROWS)
    row = lax.broadcasted_iota(jnp.int32, (BLK, BLK), 0)
    col = lax.broadcasted_iota(jnp.int32, (BLK, BLK), 1)
    out_ref[:BLK] = jnp.where(row <= col, square_ref[...], d1)
    out_ref[BLK : 2 * BLK] = product(first, second, ROWS)
    diagonal = jnp.sum(jnp.where(row == col, d1, 0.0), axis=0, keepdims=True)
    out_ref[3 * BLK :] = jnp.broadcast_to(diagonal, (8, BLK))
    after = centred(message_ref[: high_ref.shape[0]])
    out_ref[2 * BLK : 3 * BLK] = product(second, after, ROWS)


LONG = pl.CostEstimate(flops=50_000_000_000, bytes_accessed=200_000_000, transcendentals=0)
TINY = pl.CostEstimate(flops=1000, bytes_accessed=1000, transcendentals=0)


def covariances(message, kept, got, last, after):
    ensemble = message.shape[0] - 8
    square = jax.ShapeDtypeStruct((BLK, BLK), jnp.float32)
    half = jax.ShapeDtypeStruct((ensemble, BLK), jnp.bfloat16)
    first = pl.pallas_call(first_kernel, out_shape=(half, half, square), cost_estimate=TINY)(message)
    return pl.pallas_call(
        covariance_kernel,
        out_shape=jax.ShapeDtypeStruct((3 * BLK + 8, BLK), jnp.float32),
        cost_estimate=TINY,
    )(*first, kept, got, last, after)


def outward_kernel(message_ref, w_ref, cov_ref, out_ref):
    for level in range(out_ref.shape[0]):
        mixed = message_ref[:1, :1] * w_ref[0, level] + message_ref[:1, 1:2] * w_ref[1, level]
        out_ref[level] = product(split(mixed), split(cov_ref[level]), PLAIN)


def outward(message, w, cov):
    levels, members = w.shape[1:3]
    return pl.pallas_call(
        outward_kernel,
        grid=(1,),
        in_specs=[
            pl.BlockSpec((8, BLK), lambda i: (message.shape[0] // 8 - 1, 0)),
            pl.BlockSpec((2, levels, members, BLK), lambda i: (0, 0, 0, 1)),
            pl.BlockSpec((levels, BLK, BLK), lambda i: (0, 2, 0)),
        ],
        out_specs=pl.BlockSpec((levels, members, BLK), lambda i: (0, 0, 0)),
        out_shape=jax.ShapeDtypeStruct((levels, members, BLK), jnp.float32),
        cost_estimate=TINY,
    )(message, w, cov)


def increment_kernel(coef_ref, w_ref, wr_ref, cov_ref, kept_ref, sent_ref):
    row = lax.broadcasted_iota(jnp.int32, (BLK, BLK), 0)
    col = lax.broadcasted_iota(jnp.int32, (BLK, BLK), 1)
    here, there = slice(0, BLK), slice(BLK, 2 * BLK)
    keep = kept_ref.shape[1]
    for level in range(kept_ref.shape[0]):
        packed = cov_ref[level, :BLK]
        upper = jnp.where(row <= col, packed, 0.0)
        strict = jnp.where(row < col, packed, 0.0)
        lower = jnp.where(row > col, packed, 0.0)
        diagonal = jnp.where(row == col, cov_ref[level, 3 * BLK : 3 * BLK + 1], 0.0)
        d0 = split(upper + strict.T)
        d1 = split(lower + lower.T + diagonal)
        c01 = split(cov_ref[level, BLK : 2 * BLK])
        edge = split(cov_ref[level, 2 * BLK : 3 * BLK])

        def mixed(ref, t, j, part=slice(None)):
            at = t * 6 + j * 2
            return split(
                coef_ref[at] * ref[0, level, :, part] + coef_ref[at + 1] * ref[1, level, :, part]
            )

        zero = product(mixed(w_ref, 0, 1, here), d0, PLAIN) + product(
            mixed(w_ref, 0, 2, there), c01, LANES
        )
        one = (
            product(mixed(w_ref, 1, 0, here), c01, PLAIN)
            + product(mixed(w_ref, 1, 1, there), d1, PLAIN)
            + product(mixed(wr_ref, 1, 2), edge, LANES)
        )
        for ref, rows in ((kept_ref, slice(0, keep)), (sent_ref, slice(keep, 2 * keep))):
            ref[level, :, here] = zero[rows]
            ref[level, :, there] = one[rows]


def increments(coefs, w, w_right, cov):
    levels, members = w.shape[1:3]
    half = jax.ShapeDtypeStruct((levels, members // 2, 2 * BLK), jnp.float32)
    vmem = pl.BlockSpec(memory_space=pltpu.VMEM)
    return pl.pallas_call(
        increment_kernel,
        in_specs=[pl.BlockSpec(memory_space=pltpu.SMEM), vmem, vmem, vmem],
        out_specs=(vmem, vmem),
        out_shape=(half, half),
        cost_estimate=TINY,
    )(coefs, w, w_right, cov)


def gather_kernel(mine_ref, got_ref, w_ref, low_ref):
    keep = mine_ref.shape[2]
    for ref, rows in ((mine_ref, slice(0, keep)), (got_ref, slice(keep, 2 * keep))):
        w_ref[0, :, rows] = ref[0]
        low_ref[0, :, rows] = ref[0, :, :, :BLK]


def gathered(mine, got):
    batches, levels, members, width = mine.shape
    block = lambda m, c: pl.BlockSpec((1, levels, m, c), lambda i: (i, 0, 0, 0))
    shape = lambda c: jax.ShapeDtypeStruct((batches, levels, 2 * members, c), jnp.float32)
    return pl.pallas_call(
        gather_kernel,
        grid=(batches,),
        in_specs=[block(members, width)] * 2,
        out_specs=(block(2 * members, width), block(2 * members, BLK)),
        out_shape=(shape(width), shape(BLK)),
        cost_estimate=LONG,
    )(mine, got)


def one_hot(index, count):
    return (index[:, None] == jnp.arange(count, dtype=jnp.int32)[None, :]).astype(jnp.float32)


def pick(x, index):
    return lax.dynamic_index_in_dim(x, index, 0, keepdims=False)


def local(members, weights, taper_table, pair_blocks, pair_taper, pair_batch):
    member_loc, levels, column_count = members.shape
    ensemble = member_loc * lax.axis_size("member")
    regions = lax.axis_size("region")
    right = [(i, (i + 1) % regions) for i in range(regions)]
    left = [(j, i) for i, j in right]
    me = lax.axis_index("member")
    chip, core = me // 2, me % 2
    half = levels // 2

    states = jnp.transpose(members, (1, 0, 2))
    mine = lax.dynamic_slice_in_dim(states, core * half, half, 0)
    theirs = lax.dynamic_slice_in_dim(states, (1 - core) * half, half, 0)
    theirs, weights = lax.optimization_barrier((theirs, weights))
    states = jnp.concatenate([mine, lax.ppermute(theirs, "member", SWAP)], axis=1)

    near = chip ^ 1
    cross = CHIPS - 1 - chip
    one = jnp.where(core == 0, near, cross)
    two = jnp.where(core == 0, cross, near)
    both = CHIPS - 1 - near
    step_one, step_two = pairing(0), pairing(1)

    def to_owner(block):
        x = states[:, :, block * BLK : (block + 1) * BLK]
        got = lax.ppermute(jnp.stack([pick(x, one), pick(x, both)]), "member", step_one)
        last = lax.ppermute(jnp.stack([pick(x, two), got[1]]), "member", step_two)
        return pick(x, chip), got[0], last.reshape(-1, BLK)

    first, second = to_owner(0), to_owner(1)
    taken, pair_taper = lax.optimization_barrier((first[1], pair_taper))
    first = first[0], taken, first[2]
    tapers = jnp.dot(
        one_hot(pair_taper, taper_table.shape[0]), taper_table, precision=lax.Precision.HIGHEST
    ) / (ensemble - 1)
    targets = pair_blocks[:, 0]
    slot = targets * 6 + (pair_blocks[:, 1] - targets) * 2 + pair_batch
    coefs = jnp.sum(one_hot(slot, 12) * tapers[:, None], axis=0)
    rows = jnp.pad(coefs[None], ((0, 7), (0, BLK - 12)))
    message = jnp.concatenate([*first, rows])
    after = lax.ppermute(message, "region", left)

    w = jnp.transpose(weights, (0, 2, 1, 3))
    mine = lax.dynamic_slice_in_dim(w, core * half, half, 1)
    theirs = lax.dynamic_slice_in_dim(w, (1 - core) * half, half, 1)
    w, low = gathered(mine, lax.ppermute(theirs, "member", SWAP))
    w_right = lax.ppermute(low, "region", left)

    own = covariances(message, *second, after)
    cov = lax.all_gather(own, "member", axis_index_groups=GROUPS)
    from_left = lax.ppermute(outward(after, w, cov), "region", right)
    kept, sent = increments(coefs, w, w_right, cov)
    from_left = jnp.pad(from_left, ((0, 0), (0, 0), (0, column_count - BLK)))
    kept, sent = kept + from_left[:, :member_loc], sent + from_left[:, member_loc:]
    came = lax.ppermute(sent, "member", SWAP)
    change = jnp.where(
        core == 0, jnp.concatenate([kept, came]), jnp.concatenate([came, kept])
    )
    return members + jnp.transpose(change, (1, 0, 2))


def solution(mesh):
    placed = (
        P("member", None, "region"),
        P(None, "member", None, "region"),
        P(),
        P("region", None),
        P("region"),
        P("region"),
    )
    return jax.shard_map(
        local, mesh=mesh, in_specs=placed, out_specs=P("member", None, "region"), check_vma=False
    )
```

```python
import functools

import jax
import jax.numpy as jnp
from jax import lax
from jax.experimental import pallas as pl
from jax.experimental.pallas import tpu as pltpu
from jax.sharding import PartitionSpec as P

BLK = 128
CHIPS = 4
GROUPS = [[2 * z + c for z in range(CHIPS)] for c in range(2)]
SWAP = [(i, i ^ 1) for i in range(2 * CHIPS)]
NEAR = [z ^ 1 for z in range(CHIPS)]
CROSS = [CHIPS - 1 - z for z in range(CHIPS)]


def pairing(step):
    moves = []
    for z in range(CHIPS):
        for core in range(2):
            partner = (NEAR if (core + step) % 2 == 0 else CROSS)[z]
            moves.append((2 * z + core, 2 * partner + core))
    return moves


def split(x):
    high = x.astype(jnp.bfloat16)
    return high, (x - high.astype(jnp.float32)).astype(jnp.bfloat16)


def product(a, b, dims):
    (ah, al), (bh, bl) = a, b
    dot = functools.partial(
        lax.dot_general, dimension_numbers=(dims, ((), ())), preferred_element_type=jnp.float32
    )
    return dot(ah, bh) + (dot(ah, bl) + dot(al, bh))


ROWS = ((0,), (0,))
PLAIN = ((1,), (0,))
LANES = ((1,), (1,))


def centred(*parts):
    count = sum(p.shape[0] for p in parts)
    mean = sum(jnp.sum(p, axis=0, keepdims=True) for p in parts) / count
    return split(jnp.concatenate([p - mean for p in parts], axis=0))


def first_kernel(message_ref, high_ref, low_ref, square_ref):
    first = centred(message_ref[: high_ref.shape[0]])
    high_ref[...], low_ref[...] = first
    square_ref[...] = product(first, first, ROWS)


def covariance_kernel(
    high_ref, low_ref, square_ref, kept_ref, got_ref, last_ref, message_ref, ahead_ref, out_ref
):
    second = centred(kept_ref[...], got_ref[...], last_ref[...])
    first = high_ref[...], low_ref[...]
    d1 = product(second, second, ROWS)
    row = lax.broadcasted_iota(jnp.int32, (BLK, BLK), 0)
    col = lax.broadcasted_iota(jnp.int32, (BLK, BLK), 1)
    out_ref[:BLK] = jnp.where(row <= col, square_ref[...], d1)
    out_ref[BLK : 2 * BLK] = product(first, second, ROWS)
    diagonal = jnp.sum(jnp.where(row == col, d1, 0.0), axis=0, keepdims=True)
    out_ref[3 * BLK :] = jnp.broadcast_to(diagonal, (8, BLK))
    after = centred(message_ref[: high_ref.shape[0]])
    out_ref[2 * BLK : 3 * BLK] = product(second, after, ROWS)


LONG = pl.CostEstimate(flops=50_000_000_000, bytes_accessed=200_000_000, transcendentals=0)
TINY = pl.CostEstimate(flops=1000, bytes_accessed=1000, transcendentals=0)


def covariances(message, kept, got, last, after, ahead):
    ensemble = message.shape[0] - 8
    square = jax.ShapeDtypeStruct((BLK, BLK), jnp.float32)
    half = jax.ShapeDtypeStruct((ensemble, BLK), jnp.bfloat16)
    first = pl.pallas_call(first_kernel, out_shape=(half, half, square), cost_estimate=LONG)(message)
    return pl.pallas_call(
        covariance_kernel,
        in_specs=[pl.BlockSpec(memory_space=pltpu.VMEM)] * 7 + [pl.BlockSpec(memory_space=pl.ANY)],
        out_shape=jax.ShapeDtypeStruct((3 * BLK + 8, BLK), jnp.float32),
        cost_estimate=TINY,
    )(*first, kept, got, last, after, ahead)


def outward_kernel(message_ref, w_ref, cov_ref, out_ref):
    for level in range(out_ref.shape[0]):
        mixed = message_ref[:1, :1] * w_ref[0, level] + message_ref[:1, 1:2] * w_ref[1, level]
        out_ref[level] = product(split(mixed), split(cov_ref[level]), PLAIN)


def outward(message, w, cov):
    levels, members = w.shape[1:3]
    return pl.pallas_call(
        outward_kernel,
        grid=(1,),
        in_specs=[
            pl.BlockSpec((8, BLK), lambda i: (message.shape[0] // 8 - 1, 0)),
            pl.BlockSpec((2, levels, members, BLK), lambda i: (0, 0, 0, 1)),
            pl.BlockSpec((levels, BLK, BLK), lambda i: (0, 2, 0)),
        ],
        out_specs=pl.BlockSpec((levels, members, BLK), lambda i: (0, 0, 0)),
        out_shape=jax.ShapeDtypeStruct((levels, members, BLK), jnp.float32),
        cost_estimate=TINY,
    )(message, w, cov)


def increment_kernel(coef_ref, w_ref, wr_ref, cov_ref, kept_ref, sent_ref):
    row = lax.broadcasted_iota(jnp.int32, (BLK, BLK), 0)
    col = lax.broadcasted_iota(jnp.int32, (BLK, BLK), 1)
    here, there = slice(0, BLK), slice(BLK, 2 * BLK)
    keep = kept_ref.shape[1]
    for level in range(kept_ref.shape[0]):
        packed = cov_ref[level, :BLK]
        upper = jnp.where(row <= col, packed, 0.0)
        strict = jnp.where(row < col, packed, 0.0)
        lower = jnp.where(row > col, packed, 0.0)
        diagonal = jnp.where(row == col, cov_ref[level, 3 * BLK : 3 * BLK + 1], 0.0)
        d0 = split(upper + strict.T)
        d1 = split(lower + lower.T + diagonal)
        c01 = split(cov_ref[level, BLK : 2 * BLK])
        edge = split(cov_ref[level, 2 * BLK : 3 * BLK])

        def mixed(ref, t, j, part=slice(None)):
            at = t * 6 + j * 2
            return split(
                coef_ref[at] * ref[0, level, :, part] + coef_ref[at + 1] * ref[1, level, :, part]
            )

        zero = product(mixed(w_ref, 0, 1, here), d0, PLAIN) + product(
            mixed(w_ref, 0, 2, there), c01, LANES
        )
        one = (
            product(mixed(w_ref, 1, 0, here), c01, PLAIN)
            + product(mixed(w_ref, 1, 1, there), d1, PLAIN)
            + product(mixed(wr_ref, 1, 2), edge, LANES)
        )
        for ref, rows in ((kept_ref, slice(0, keep)), (sent_ref, slice(keep, 2 * keep))):
            ref[level, :, here] = zero[rows]
            ref[level, :, there] = one[rows]


def increments(coefs, w, w_right, cov):
    levels, members = w.shape[1:3]
    half = jax.ShapeDtypeStruct((levels, members // 2, 2 * BLK), jnp.float32)
    vmem = pl.BlockSpec(memory_space=pltpu.VMEM)
    return pl.pallas_call(
        increment_kernel,
        in_specs=[pl.BlockSpec(memory_space=pltpu.SMEM), vmem, vmem, vmem],
        out_specs=(vmem, vmem),
        out_shape=(half, half),
        cost_estimate=TINY,
    )(coefs, w, w_right, cov)


def gather_kernel(mine_ref, got_ref, w_ref, low_ref):
    keep = mine_ref.shape[2]
    for ref, rows in ((mine_ref, slice(0, keep)), (got_ref, slice(keep, 2 * keep))):
        w_ref[0, :, rows] = ref[0]
        low_ref[0, :, rows] = ref[0, :, :, :BLK]


def gathered(mine, got):
    batches, levels, members, width = mine.shape
    block = lambda m, c: pl.BlockSpec((1, levels, m, c), lambda i: (i, 0, 0, 0))
    shape = lambda c: jax.ShapeDtypeStruct((batches, levels, 2 * members, c), jnp.float32)
    return pl.pallas_call(
        gather_kernel,
        grid=(batches,),
        in_specs=[block(members, width)] * 2,
        out_specs=(block(2 * members, width), block(2 * members, BLK)),
        out_shape=(shape(width), shape(BLK)),
        cost_estimate=LONG,
    )(mine, got)


def one_hot(index, count):
    return (index[:, None] == jnp.arange(count, dtype=jnp.int32)[None, :]).astype(jnp.float32)


def pick(x, index):
    return lax.dynamic_index_in_dim(x, index, 0, keepdims=False)


def local(members, weights, taper_table, pair_blocks, pair_taper, pair_batch):
    member_loc, levels, column_count = members.shape
    ensemble = member_loc * lax.axis_size("member")
    regions = lax.axis_size("region")
    right = [(i, (i + 1) % regions) for i in range(regions)]
    left = [(j, i) for i, j in right]
    me = lax.axis_index("member")
    chip, core = me // 2, me % 2
    half = levels // 2

    states = jnp.transpose(members, (1, 0, 2))
    mine = lax.dynamic_slice_in_dim(states, core * half, half, 0)
    theirs = lax.dynamic_slice_in_dim(states, (1 - core) * half, half, 0)
    theirs, weights = lax.optimization_barrier((theirs, weights))
    states = jnp.concatenate([mine, lax.ppermute(theirs, "member", SWAP)], axis=1)

    near = chip ^ 1
    cross = CHIPS - 1 - chip
    one = jnp.where(core == 0, near, cross)
    two = jnp.where(core == 0, cross, near)
    both = CHIPS - 1 - near
    step_one, step_two = pairing(0), pairing(1)

    def to_owner(block):
        x = states[:, :, block * BLK : (block + 1) * BLK]
        got = lax.ppermute(jnp.stack([pick(x, one), pick(x, both)]), "member", step_one)
        last = lax.ppermute(jnp.stack([pick(x, two), got[1]]), "member", step_two)
        return pick(x, chip), got[0], last.reshape(-1, BLK)

    first, second = to_owner(0), to_owner(1)
    taken, pair_taper = lax.optimization_barrier((first[1], pair_taper))
    first = first[0], taken, first[2]
    tapers = jnp.dot(
        one_hot(pair_taper, taper_table.shape[0]), taper_table, precision=lax.Precision.HIGHEST
    ) / (ensemble - 1)
    targets = pair_blocks[:, 0]
    slot = targets * 6 + (pair_blocks[:, 1] - targets) * 2 + pair_batch
    coefs = jnp.sum(one_hot(slot, 12) * tapers[:, None], axis=0)
    rows = jnp.pad(coefs[None], ((0, 7), (0, BLK - 12)))
    message = jnp.concatenate([*first, rows])
    after = lax.ppermute(message, "region", left)

    w = jnp.transpose(weights, (0, 2, 1, 3))
    mine = lax.dynamic_slice_in_dim(w, core * half, half, 1)
    theirs = lax.dynamic_slice_in_dim(w, (1 - core) * half, half, 1)
    w, low = gathered(mine, lax.ppermute(theirs, "member", SWAP))
    w_right = lax.ppermute(low, "region", left)

    own = covariances(message, *second, after, w_right)
    cov = lax.all_gather(own, "member", axis_index_groups=GROUPS)
    from_left = lax.ppermute(outward(after, w, cov), "region", right)
    kept, sent = increments(coefs, w, w_right, cov)
    from_left = jnp.pad(from_left, ((0, 0), (0, 0), (0, column_count - BLK)))
    kept, sent = kept + from_left[:, :member_loc], sent + from_left[:, member_loc:]
    came = lax.ppermute(sent, "member", SWAP)
    change = jnp.where(
        core == 0, jnp.concatenate([kept, came]), jnp.concatenate([came, kept])
    )
    return members + jnp.transpose(change, (1, 0, 2))


def solution(mesh):
    placed = (
        P("member", None, "region"),
        P(None, "member", None, "region"),
        P(),
        P("region", None),
        P("region"),
        P("region"),
    )
    return jax.shard_map(
        local, mesh=mesh, in_specs=placed, out_specs=P("member", None, "region"), check_vma=False
    )
```

```python
import functools

import jax
import jax.numpy as jnp
from jax import lax
from jax.experimental import pallas as pl
from jax.experimental.pallas import tpu as pltpu
from jax.sharding import PartitionSpec as P

BLK = 128
CHIPS = 4
GROUPS = [[2 * z + c for z in range(CHIPS)] for c in range(2)]
SWAP = [(i, i ^ 1) for i in range(2 * CHIPS)]
NEAR = [z ^ 1 for z in range(CHIPS)]
CROSS = [CHIPS - 1 - z for z in range(CHIPS)]


def pairing(step):
    moves = []
    for z in range(CHIPS):
        for core in range(2):
            partner = (NEAR if (core + step) % 2 == 0 else CROSS)[z]
            moves.append((2 * z + core, 2 * partner + core))
    return moves


def split(x):
    high = x.astype(jnp.bfloat16)
    return high, (x - high.astype(jnp.float32)).astype(jnp.bfloat16)


def product(a, b, dims):
    (ah, al), (bh, bl) = a, b
    dot = functools.partial(
        lax.dot_general, dimension_numbers=(dims, ((), ())), preferred_element_type=jnp.float32
    )
    return dot(ah, bh) + (dot(ah, bl) + dot(al, bh))


ROWS = ((0,), (0,))
PLAIN = ((1,), (0,))
LANES = ((1,), (1,))


def centred(*parts):
    count = sum(p.shape[0] for p in parts)
    mean = sum(jnp.sum(p, axis=0, keepdims=True) for p in parts) / count
    return split(jnp.concatenate([p - mean for p in parts], axis=0))


def first_kernel(message_ref, high_ref, low_ref, square_ref):
    first = centred(message_ref[: high_ref.shape[0]])
    high_ref[...], low_ref[...] = first
    square_ref[...] = product(first, first, ROWS)


def covariance_kernel(
    high_ref, low_ref, square_ref, kept_ref, got_ref, last_ref, message_ref, out_ref
):
    second = centred(kept_ref[...], got_ref[...], last_ref[...])
    first = high_ref[...], low_ref[...]
    d1 = product(second, second, ROWS)
    row = lax.broadcasted_iota(jnp.int32, (BLK, BLK), 0)
    col = lax.broadcasted_iota(jnp.int32, (BLK, BLK), 1)
    out_ref[:BLK] = jnp.where(row <= col, square_ref[...], d1)
    out_ref[BLK : 2 * BLK] = product(first, second, ROWS)
    diagonal = jnp.sum(jnp.where(row == col, d1, 0.0), axis=0, keepdims=True)
    out_ref[3 * BLK :] = jnp.broadcast_to(diagonal, (8, BLK))
    after = centred(message_ref[: high_ref.shape[0]])
    out_ref[2 * BLK : 3 * BLK] = product(second, after, ROWS)


LONG = pl.CostEstimate(flops=50_000_000_000, bytes_accessed=200_000_000, transcendentals=0)
TINY = pl.CostEstimate(flops=1000, bytes_accessed=1000, transcendentals=0)


def covariances(message, kept, got, last, after):
    ensemble = message.shape[0] - 8
    square = jax.ShapeDtypeStruct((BLK, BLK), jnp.float32)
    half = jax.ShapeDtypeStruct((ensemble, BLK), jnp.bfloat16)
    first = pl.pallas_call(first_kernel, out_shape=(half, half, square), cost_estimate=LONG)(message)
    return pl.pallas_call(
        covariance_kernel,
        out_shape=jax.ShapeDtypeStruct((3 * BLK + 8, BLK), jnp.float32),
        cost_estimate=TINY,
    )(*first, kept, got, last, after)


def outward_kernel(message_ref, w_ref, cov_ref, out_ref):
    for level in range(out_ref.shape[0]):
        mixed = message_ref[:1, :1] * w_ref[0, level] + message_ref[:1, 1:2] * w_ref[1, level]
        out_ref[level] = product(split(mixed), split(cov_ref[level]), PLAIN)


def outward(message, w, cov):
    levels, members = w.shape[1:3]
    return pl.pallas_call(
        outward_kernel,
        grid=(1,),
        in_specs=[
            pl.BlockSpec((8, BLK), lambda i: (message.shape[0] // 8 - 1, 0)),
            pl.BlockSpec((2, levels, members, BLK), lambda i: (0, 0, 0, 1)),
            pl.BlockSpec((levels, BLK, BLK), lambda i: (0, 2, 0)),
        ],
        out_specs=pl.BlockSpec((levels, members, BLK), lambda i: (0, 0, 0)),
        out_shape=jax.ShapeDtypeStruct((levels, members, BLK), jnp.float32),
        cost_estimate=TINY,
    )(message, w, cov)


def increment_kernel(coef_ref, w_ref, wr_ref, cov_ref, kept_ref, sent_ref):
    row = lax.broadcasted_iota(jnp.int32, (BLK, BLK), 0)
    col = lax.broadcasted_iota(jnp.int32, (BLK, BLK), 1)
    here, there = slice(0, BLK), slice(BLK, 2 * BLK)
    keep = kept_ref.shape[1]
    for level in range(kept_ref.shape[0]):
        packed = cov_ref[level, :BLK]
        upper = jnp.where(row <= col, packed, 0.0)
        strict = jnp.where(row < col, packed, 0.0)
        lower = jnp.where(row > col, packed, 0.0)
        diagonal = jnp.where(row == col, cov_ref[level, 3 * BLK : 3 * BLK + 1], 0.0)
        d0 = split(upper + strict.T)
        d1 = split(lower + lower.T + diagonal)
        c01 = split(cov_ref[level, BLK : 2 * BLK])
        edge = split(cov_ref[level, 2 * BLK : 3 * BLK])

        def mixed(ref, t, j, part=slice(None)):
            at = t * 6 + j * 2
            return split(
                coef_ref[at] * ref[0, level, :, part] + coef_ref[at + 1] * ref[1, level, :, part]
            )

        zero = product(mixed(w_ref, 0, 1, here), d0, PLAIN) + product(
            mixed(w_ref, 0, 2, there), c01, LANES
        )
        one = (
            product(mixed(w_ref, 1, 0, here), c01, PLAIN)
            + product(mixed(w_ref, 1, 1, there), d1, PLAIN)
            + product(mixed(wr_ref, 1, 2), edge, LANES)
        )
        for ref, rows in ((kept_ref, slice(0, keep)), (sent_ref, slice(keep, 2 * keep))):
            ref[level, :, here] = zero[rows]
            ref[level, :, there] = one[rows]


def increments(coefs, w, w_right, cov):
    levels, members = w.shape[1:3]
    half = jax.ShapeDtypeStruct((levels, members // 2, 2 * BLK), jnp.float32)
    vmem = pl.BlockSpec(memory_space=pltpu.VMEM)
    return pl.pallas_call(
        increment_kernel,
        in_specs=[pl.BlockSpec(memory_space=pltpu.SMEM), vmem, vmem, vmem],
        out_specs=(vmem, vmem),
        out_shape=(half, half),
        cost_estimate=TINY,
    )(coefs, w, w_right, cov)


def gather_kernel(mine_ref, got_ref, w_ref, low_ref):
    keep = mine_ref.shape[2]
    for ref, rows in ((mine_ref, slice(0, keep)), (got_ref, slice(keep, 2 * keep))):
        w_ref[0, :, rows] = ref[0]
        low_ref[0, :, rows] = ref[0, :, :, :BLK]


def gathered(mine, got):
    batches, levels, members, width = mine.shape
    block = lambda m, c: pl.BlockSpec((1, levels, m, c), lambda i: (i, 0, 0, 0))
    shape = lambda c: jax.ShapeDtypeStruct((batches, levels, 2 * members, c), jnp.float32)
    return pl.pallas_call(
        gather_kernel,
        grid=(batches,),
        in_specs=[block(members, width)] * 2,
        out_specs=(block(2 * members, width), block(2 * members, BLK)),
        out_shape=(shape(width), shape(BLK)),
        cost_estimate=LONG,
    )(mine, got)


def one_hot(index, count):
    return (index[:, None] == jnp.arange(count, dtype=jnp.int32)[None, :]).astype(jnp.float32)


def pick(x, index):
    return lax.dynamic_index_in_dim(x, index, 0, keepdims=False)


def local(members, weights, taper_table, pair_blocks, pair_taper, pair_batch):
    member_loc, levels, column_count = members.shape
    ensemble = member_loc * lax.axis_size("member")
    regions = lax.axis_size("region")
    right = [(i, (i + 1) % regions) for i in range(regions)]
    left = [(j, i) for i, j in right]
    me = lax.axis_index("member")
    chip, core = me // 2, me % 2
    half = levels // 2

    states = jnp.transpose(members, (1, 0, 2))
    mine = lax.dynamic_slice_in_dim(states, core * half, half, 0)
    theirs = lax.dynamic_slice_in_dim(states, (1 - core) * half, half, 0)
    theirs, weights = lax.optimization_barrier((theirs, weights))
    states = jnp.concatenate([mine, lax.ppermute(theirs, "member", SWAP)], axis=1)

    near = chip ^ 1
    cross = CHIPS - 1 - chip
    one = jnp.where(core == 0, near, cross)
    two = jnp.where(core == 0, cross, near)
    both = CHIPS - 1 - near
    step_one, step_two = pairing(0), pairing(1)

    def to_owner(block):
        x = states[:, :, block * BLK : (block + 1) * BLK]
        got = lax.ppermute(jnp.stack([pick(x, one), pick(x, both)]), "member", step_one)
        last = lax.ppermute(jnp.stack([pick(x, two), got[1]]), "member", step_two)
        return pick(x, chip), got[0], last.reshape(-1, BLK)

    first, second = to_owner(0), to_owner(1)
    taken, pair_taper = lax.optimization_barrier((first[1], pair_taper))
    first = first[0], taken, first[2]
    tapers = jnp.dot(
        one_hot(pair_taper, taper_table.shape[0]), taper_table, precision=lax.Precision.HIGHEST
    ) / (ensemble - 1)
    targets = pair_blocks[:, 0]
    slot = targets * 6 + (pair_blocks[:, 1] - targets) * 2 + pair_batch
    coefs = jnp.sum(one_hot(slot, 12) * tapers[:, None], axis=0)
    rows = jnp.pad(coefs[None], ((0, 7), (0, BLK - 12)))
    w = jnp.transpose(weights, (0, 2, 1, 3))
    mine = lax.dynamic_slice_in_dim(w, core * half, half, 1)
    theirs = lax.dynamic_slice_in_dim(w, (1 - core) * half, half, 1)
    w, low = gathered(mine, lax.ppermute(theirs, "member", SWAP))
    rows, low = lax.optimization_barrier((rows, low))
    message = jnp.concatenate([*first, rows])
    after = lax.ppermute(message, "region", left)

    w_right = lax.ppermute(low, "region", left)

    own = covariances(message, *second, after)
    cov = lax.all_gather(own, "member", axis_index_groups=GROUPS)
    from_left = lax.ppermute(outward(after, w, cov), "region", right)
    kept, sent = increments(coefs, w, w_right, cov)
    from_left = jnp.pad(from_left, ((0, 0), (0, 0), (0, column_count - BLK)))
    kept, sent = kept + from_left[:, :member_loc], sent + from_left[:, member_loc:]
    came = lax.ppermute(sent, "member", SWAP)
    change = jnp.where(
        core == 0, jnp.concatenate([kept, came]), jnp.concatenate([came, kept])
    )
    return members + jnp.transpose(change, (1, 0, 2))


def solution(mesh):
    placed = (
        P("member", None, "region"),
        P(None, "member", None, "region"),
        P(),
        P("region", None),
        P("region"),
        P("region"),
    )
    return jax.shard_map(
        local, mesh=mesh, in_specs=placed, out_specs=P("member", None, "region"), check_vma=False
    )
```

```python
import functools

import jax
import jax.numpy as jnp
from jax import lax
from jax.experimental import pallas as pl
from jax.experimental.pallas import tpu as pltpu
from jax.sharding import PartitionSpec as P

BLK = 128
CHIPS = 4
SWAP = [(i, i ^ 1) for i in range(2 * CHIPS)]
NEAR = [z ^ 1 for z in range(CHIPS)]
CROSS = [CHIPS - 1 - z for z in range(CHIPS)]


def pairing(step):
    moves = []
    for z in range(CHIPS):
        for core in range(2):
            partner = (NEAR if (core + step) % 2 == 0 else CROSS)[z]
            moves.append((2 * z + core, 2 * partner + core))
    return moves


def split(x):
    high = x.astype(jnp.bfloat16)
    return high, (x - high.astype(jnp.float32)).astype(jnp.bfloat16)


def product(a, b, dims):
    (ah, al), (bh, bl) = a, b
    dot = functools.partial(
        lax.dot_general, dimension_numbers=(dims, ((), ())), preferred_element_type=jnp.float32
    )
    return dot(ah, bh) + (dot(ah, bl) + dot(al, bh))


ROWS = ((0,), (0,))
PLAIN = ((1,), (0,))
LANES = ((1,), (1,))


def centred(*parts):
    count = sum(p.shape[0] for p in parts)
    mean = sum(jnp.sum(p, axis=0, keepdims=True) for p in parts) / count
    return split(jnp.concatenate([p - mean for p in parts], axis=0))


def first_kernel(message_ref, high_ref, low_ref, square_ref):
    first = centred(message_ref[: high_ref.shape[0]])
    high_ref[...], low_ref[...] = first
    square_ref[...] = product(first, first, ROWS)


def covariance_kernel(
    high_ref, low_ref, square_ref, kept_ref, got_ref, last_ref, message_ref, edge_ref, own_ref
):
    second = centred(kept_ref[...], got_ref[...], last_ref[...])
    first = high_ref[...], low_ref[...]
    d1 = product(second, second, ROWS)
    row = lax.broadcasted_iota(jnp.int32, (BLK, BLK), 0)
    col = lax.broadcasted_iota(jnp.int32, (BLK, BLK), 1)
    own_ref[:BLK] = jnp.where(row <= col, square_ref[...], d1)
    own_ref[BLK : 2 * BLK] = product(first, second, ROWS)
    diagonal = jnp.sum(jnp.where(row == col, d1, 0.0), axis=0, keepdims=True)
    own_ref[2 * BLK :] = jnp.broadcast_to(diagonal, (8, BLK))
    after = centred(message_ref[: high_ref.shape[0]])
    edge_ref[...] = product(second, after, ROWS)


LONG = pl.CostEstimate(flops=50_000_000_000, bytes_accessed=200_000_000, transcendentals=0)
TINY = pl.CostEstimate(flops=1000, bytes_accessed=1000, transcendentals=0)


def covariances(message, kept, got, last, after):
    ensemble = message.shape[0] - 8
    square = jax.ShapeDtypeStruct((BLK, BLK), jnp.float32)
    half = jax.ShapeDtypeStruct((ensemble, BLK), jnp.bfloat16)
    first = pl.pallas_call(first_kernel, out_shape=(half, half, square), cost_estimate=LONG)(message)
    return pl.pallas_call(
        covariance_kernel,
        out_shape=(square, jax.ShapeDtypeStruct((2 * BLK + 8, BLK), jnp.float32)),
        cost_estimate=TINY,
    )(*first, kept, got, last, after)


def pieces(own_ref, near_ref, far_ref):
    return own_ref[...], near_ref[...], far_ref[0], far_ref[1]


def outward_kernel(order_ref, message_ref, w_ref, own_ref, near_ref, far_ref, out_ref):
    for step, edge in enumerate(pieces(own_ref, near_ref, far_ref)):
        level = order_ref[step]
        mixed = message_ref[:1, :1] * w_ref[0, level] + message_ref[:1, 1:2] * w_ref[1, level]
        out_ref[level] = product(split(mixed), split(edge), PLAIN)


def outward(order, message, w, edges):
    levels, members = w.shape[1:3]
    whole = lambda x: pl.BlockSpec(x.shape, lambda i: (0,) * x.ndim)
    return pl.pallas_call(
        outward_kernel,
        grid=(1,),
        in_specs=[
            pl.BlockSpec(memory_space=pltpu.SMEM),
            pl.BlockSpec((8, BLK), lambda i: (message.shape[0] // 8 - 1, 0)),
            pl.BlockSpec((2, levels, members, BLK), lambda i: (0, 0, 0, 1)),
            *(whole(x) for x in edges),
        ],
        out_specs=pl.BlockSpec((levels, members, BLK), lambda i: (0, 0, 0)),
        out_shape=jax.ShapeDtypeStruct((levels, members, BLK), jnp.float32),
        cost_estimate=LONG,
    )(order, message, w, *edges)


def increment_kernel(
    coef_ref, order_ref, w_ref, wr_ref, e0_ref, e1_ref, e2_ref, c0_ref, c1_ref, c2_ref, kept_ref, sent_ref
):
    row = lax.broadcasted_iota(jnp.int32, (BLK, BLK), 0)
    col = lax.broadcasted_iota(jnp.int32, (BLK, BLK), 1)
    here, there = slice(0, BLK), slice(BLK, 2 * BLK)
    keep = kept_ref.shape[1]
    found = zip(pieces(e0_ref, e1_ref, e2_ref), pieces(c0_ref, c1_ref, c2_ref))
    for step, (edge, cov) in enumerate(found):
        level = order_ref[step]
        packed = cov[:BLK]
        upper = jnp.where(row <= col, packed, 0.0)
        strict = jnp.where(row < col, packed, 0.0)
        lower = jnp.where(row > col, packed, 0.0)
        diagonal = jnp.where(row == col, cov[2 * BLK : 2 * BLK + 1], 0.0)
        d0 = split(upper + strict.T)
        d1 = split(lower + lower.T + diagonal)
        c01 = split(cov[BLK : 2 * BLK])

        def mixed(ref, t, j, part=slice(None)):
            at = t * 6 + j * 2
            return split(
                coef_ref[at] * ref[0, level, :, part] + coef_ref[at + 1] * ref[1, level, :, part]
            )

        zero = product(mixed(w_ref, 0, 1, here), d0, PLAIN) + product(
            mixed(w_ref, 0, 2, there), c01, LANES
        )
        one = (
            product(mixed(w_ref, 1, 0, here), c01, PLAIN)
            + product(mixed(w_ref, 1, 1, there), d1, PLAIN)
            + product(mixed(wr_ref, 1, 2), split(edge), LANES)
        )
        for ref, rows in ((kept_ref, slice(0, keep)), (sent_ref, slice(keep, 2 * keep))):
            ref[level, :, here] = zero[rows]
            ref[level, :, there] = one[rows]


def increments(coefs, order, w, w_right, edges, covs):
    levels, members = w.shape[1:3]
    half = jax.ShapeDtypeStruct((levels, members // 2, 2 * BLK), jnp.float32)
    vmem, smem = (pl.BlockSpec(memory_space=m) for m in (pltpu.VMEM, pltpu.SMEM))
    return pl.pallas_call(
        increment_kernel,
        in_specs=[smem, smem] + [vmem] * 8,
        out_specs=(vmem, vmem),
        out_shape=(half, half),
        cost_estimate=TINY,
    )(coefs, order, w, w_right, *edges, *covs)


def gather_kernel(mine_ref, got_ref, w_ref, low_ref):
    keep = mine_ref.shape[2]
    for ref, rows in ((mine_ref, slice(0, keep)), (got_ref, slice(keep, 2 * keep))):
        w_ref[0, :, rows] = ref[0]
        low_ref[0, :, rows] = ref[0, :, :, :BLK]


def gathered(mine, got):
    batches, levels, members, width = mine.shape
    block = lambda m, c: pl.BlockSpec((1, levels, m, c), lambda i: (i, 0, 0, 0))
    shape = lambda c: jax.ShapeDtypeStruct((batches, levels, 2 * members, c), jnp.float32)
    return pl.pallas_call(
        gather_kernel,
        grid=(batches,),
        in_specs=[block(members, width)] * 2,
        out_specs=(block(2 * members, width), block(2 * members, BLK)),
        out_shape=(shape(width), shape(BLK)),
        cost_estimate=LONG,
    )(mine, got)


def one_hot(index, count):
    return (index[:, None] == jnp.arange(count, dtype=jnp.int32)[None, :]).astype(jnp.float32)


def pick(x, index):
    return lax.dynamic_index_in_dim(x, index, 0, keepdims=False)


def local(members, weights, taper_table, pair_blocks, pair_taper, pair_batch):
    member_loc, levels, column_count = members.shape
    ensemble = member_loc * lax.axis_size("member")
    regions = lax.axis_size("region")
    right = [(i, (i + 1) % regions) for i in range(regions)]
    left = [(j, i) for i, j in right]
    me = lax.axis_index("member")
    chip, core = me // 2, me % 2
    half = levels // 2

    states = jnp.transpose(members, (1, 0, 2))
    mine = lax.dynamic_slice_in_dim(states, core * half, half, 0)
    theirs = lax.dynamic_slice_in_dim(states, (1 - core) * half, half, 0)
    theirs, weights = lax.optimization_barrier((theirs, weights))
    states = jnp.concatenate([mine, lax.ppermute(theirs, "member", SWAP)], axis=1)

    near = chip ^ 1
    cross = CHIPS - 1 - chip
    one = jnp.where(core == 0, near, cross)
    two = jnp.where(core == 0, cross, near)
    both = CHIPS - 1 - near
    step_one, step_two = pairing(0), pairing(1)

    def to_owner(block):
        x = states[:, :, block * BLK : (block + 1) * BLK]
        got = lax.ppermute(jnp.stack([pick(x, one), pick(x, both)]), "member", step_one)
        last = lax.ppermute(jnp.stack([pick(x, two), got[1]]), "member", step_two)
        return pick(x, chip), got[0], last.reshape(-1, BLK)

    first, second = to_owner(0), to_owner(1)
    taken, pair_taper = lax.optimization_barrier((second[1], pair_taper))
    second = second[0], taken, second[2]
    tapers = jnp.dot(
        one_hot(pair_taper, taper_table.shape[0]), taper_table, precision=lax.Precision.HIGHEST
    ) / (ensemble - 1)
    targets = pair_blocks[:, 0]
    slot = targets * 6 + (pair_blocks[:, 1] - targets) * 2 + pair_batch
    coefs = jnp.sum(one_hot(slot, 12) * tapers[:, None], axis=0)
    rows = jnp.pad(coefs[None], ((0, 7), (0, BLK - 12)))
    message = jnp.concatenate([*first, rows])
    after = lax.ppermute(message, "region", left)

    w = jnp.transpose(weights, (0, 2, 1, 3))
    mine = lax.dynamic_slice_in_dim(w, core * half, half, 1)
    theirs = lax.dynamic_slice_in_dim(w, (1 - core) * half, half, 1)
    w, low = gathered(mine, lax.ppermute(theirs, "member", SWAP))
    w_right = lax.ppermute(low, "region", left)

    edge, own = covariances(message, *second, after)
    order = jnp.stack([chip, one, two, both])
    edge_near = lax.ppermute(edge, "member", step_one)
    own_near = lax.ppermute(own, "member", step_one)
    edge_far = lax.ppermute(jnp.stack([edge, edge_near]), "member", step_two)
    own_far = lax.ppermute(jnp.stack([own, own_near]), "member", step_two)
    edges = edge, edge_near, edge_far
    from_left = lax.ppermute(outward(order, after, w, edges), "region", right)
    kept, sent = increments(coefs, order, w, w_right, edges, (own, own_near, own_far))
    from_left = jnp.pad(from_left, ((0, 0), (0, 0), (0, column_count - BLK)))
    kept, sent = kept + from_left[:, :member_loc], sent + from_left[:, member_loc:]
    came = lax.ppermute(sent, "member", SWAP)
    change = jnp.where(
        core == 0, jnp.concatenate([kept, came]), jnp.concatenate([came, kept])
    )
    return members + jnp.transpose(change, (1, 0, 2))


def solution(mesh):
    placed = (
        P("member", None, "region"),
        P(None, "member", None, "region"),
        P(),
        P("region", None),
        P("region"),
        P("region"),
    )
    return jax.shard_map(
        local, mesh=mesh, in_specs=placed, out_specs=P("member", None, "region"), check_vma=False
    )
```

```python
import functools

import jax
import jax.numpy as jnp
from jax import lax
from jax.experimental import pallas as pl
from jax.experimental.pallas import tpu as pltpu
from jax.sharding import PartitionSpec as P

BLK = 128
CHIPS = 4
SWAP = [(i, i ^ 1) for i in range(2 * CHIPS)]
NEAR = [z ^ 1 for z in range(CHIPS)]
CROSS = [CHIPS - 1 - z for z in range(CHIPS)]


def pairing(step):
    moves = []
    for z in range(CHIPS):
        for core in range(2):
            partner = (NEAR if (core + step) % 2 == 0 else CROSS)[z]
            moves.append((2 * z + core, 2 * partner + core))
    return moves


def split(x):
    high = x.astype(jnp.bfloat16)
    return high, (x - high.astype(jnp.float32)).astype(jnp.bfloat16)


def product(a, b, dims):
    (ah, al), (bh, bl) = a, b
    dot = functools.partial(
        lax.dot_general, dimension_numbers=(dims, ((), ())), preferred_element_type=jnp.float32
    )
    return dot(ah, bh) + (dot(ah, bl) + dot(al, bh))


ROWS = ((0,), (0,))
PLAIN = ((1,), (0,))
LANES = ((1,), (1,))


def centred(*parts):
    count = sum(p.shape[0] for p in parts)
    mean = sum(jnp.sum(p, axis=0, keepdims=True) for p in parts) / count
    return split(jnp.concatenate([p - mean for p in parts], axis=0))


def first_kernel(message_ref, high_ref, low_ref, square_ref):
    first = centred(message_ref[: high_ref.shape[0]])
    high_ref[...], low_ref[...] = first
    square_ref[...] = product(first, first, ROWS)


def covariance_kernel(
    high_ref, low_ref, square_ref, kept_ref, got_ref, last_ref, message_ref, edge_ref, own_ref
):
    second = centred(kept_ref[...], got_ref[...], last_ref[...])
    first = high_ref[...], low_ref[...]
    d1 = product(second, second, ROWS)
    row = lax.broadcasted_iota(jnp.int32, (BLK, BLK), 0)
    col = lax.broadcasted_iota(jnp.int32, (BLK, BLK), 1)
    own_ref[:BLK] = jnp.where(row <= col, square_ref[...], d1)
    own_ref[BLK : 2 * BLK] = product(first, second, ROWS)
    diagonal = jnp.sum(jnp.where(row == col, d1, 0.0), axis=0, keepdims=True)
    own_ref[2 * BLK :] = jnp.broadcast_to(diagonal, (8, BLK))
    after = centred(message_ref[: high_ref.shape[0]])
    edge_ref[...] = product(second, after, ROWS)


LONG = pl.CostEstimate(flops=50_000_000_000, bytes_accessed=200_000_000, transcendentals=0)
TINY = pl.CostEstimate(flops=1000, bytes_accessed=1000, transcendentals=0)


def covariances(message, kept, got, last, after):
    ensemble = message.shape[0] - 8
    square = jax.ShapeDtypeStruct((BLK, BLK), jnp.float32)
    half = jax.ShapeDtypeStruct((ensemble, BLK), jnp.bfloat16)
    first = pl.pallas_call(first_kernel, out_shape=(half, half, square), cost_estimate=LONG)(message)
    return pl.pallas_call(
        covariance_kernel,
        out_shape=(square, jax.ShapeDtypeStruct((2 * BLK + 8, BLK), jnp.float32)),
        cost_estimate=TINY,
    )(*first, kept, got, last, after)


def pieces(own_ref, near_ref, far_ref):
    return own_ref[...], near_ref[...], far_ref[0], far_ref[1]


def outward_kernel(order_ref, message_ref, w_ref, own_ref, near_ref, far_ref, out_ref):
    for step, edge in enumerate(pieces(own_ref, near_ref, far_ref)):
        level = order_ref[step]
        mixed = message_ref[:1, :1] * w_ref[0, level] + message_ref[:1, 1:2] * w_ref[1, level]
        out_ref[level] = product(split(mixed), split(edge), PLAIN)


def outward(order, message, w, edges):
    levels, members = w.shape[1:3]
    whole = lambda x: pl.BlockSpec(x.shape, lambda i: (0,) * x.ndim)
    return pl.pallas_call(
        outward_kernel,
        grid=(1,),
        in_specs=[
            pl.BlockSpec(memory_space=pltpu.SMEM),
            pl.BlockSpec((8, BLK), lambda i: (message.shape[0] // 8 - 1, 0)),
            pl.BlockSpec((2, levels, members, BLK), lambda i: (0, 0, 0, 1)),
            *(whole(x) for x in edges),
        ],
        out_specs=pl.BlockSpec((levels, members, BLK), lambda i: (0, 0, 0)),
        out_shape=jax.ShapeDtypeStruct((levels, members, BLK), jnp.float32),
        cost_estimate=LONG,
    )(order, message, w, *edges)


def increment_kernel(
    coef_ref, order_ref, w_ref, wr_ref, e0_ref, e1_ref, e2_ref, c0_ref, c1_ref, c2_ref, kept_ref, sent_ref
):
    row = lax.broadcasted_iota(jnp.int32, (BLK, BLK), 0)
    col = lax.broadcasted_iota(jnp.int32, (BLK, BLK), 1)
    here, there = slice(0, BLK), slice(BLK, 2 * BLK)
    keep = kept_ref.shape[1]
    found = zip(pieces(e0_ref, e1_ref, e2_ref), pieces(c0_ref, c1_ref, c2_ref))
    for step, (edge, cov) in enumerate(found):
        level = order_ref[step]
        packed = cov[:BLK]
        upper = jnp.where(row <= col, packed, 0.0)
        strict = jnp.where(row < col, packed, 0.0)
        lower = jnp.where(row > col, packed, 0.0)
        diagonal = jnp.where(row == col, cov[2 * BLK : 2 * BLK + 1], 0.0)
        d0 = split(upper + strict.T)
        d1 = split(lower + lower.T + diagonal)
        c01 = split(cov[BLK : 2 * BLK])

        def mixed(ref, t, j, part=slice(None)):
            at = t * 6 + j * 2
            return split(
                coef_ref[at] * ref[0, level, :, part] + coef_ref[at + 1] * ref[1, level, :, part]
            )

        zero = product(mixed(w_ref, 0, 1, here), d0, PLAIN) + product(
            mixed(w_ref, 0, 2, there), c01, LANES
        )
        one = (
            product(mixed(w_ref, 1, 0, here), c01, PLAIN)
            + product(mixed(w_ref, 1, 1, there), d1, PLAIN)
            + product(mixed(wr_ref, 1, 2), split(edge), LANES)
        )
        for ref, rows in ((kept_ref, slice(0, keep)), (sent_ref, slice(keep, 2 * keep))):
            ref[level, :, here] = zero[rows]
            ref[level, :, there] = one[rows]


def increments(coefs, order, w, w_right, edges, covs):
    levels, members = w.shape[1:3]
    half = jax.ShapeDtypeStruct((levels, members // 2, 2 * BLK), jnp.float32)
    vmem, smem = (pl.BlockSpec(memory_space=m) for m in (pltpu.VMEM, pltpu.SMEM))
    return pl.pallas_call(
        increment_kernel,
        in_specs=[smem, smem] + [vmem] * 8,
        out_specs=(vmem, vmem),
        out_shape=(half, half),
        cost_estimate=TINY,
    )(coefs, order, w, w_right, *edges, *covs)


def gather_kernel(mine_ref, got_ref, w_ref, low_ref):
    keep = mine_ref.shape[2]
    for ref, rows in ((mine_ref, slice(0, keep)), (got_ref, slice(keep, 2 * keep))):
        w_ref[0, :, rows] = ref[0]
        low_ref[0, :, rows] = ref[0, :, :, :BLK]


def gathered(mine, got):
    batches, levels, members, width = mine.shape
    block = lambda m, c: pl.BlockSpec((1, levels, m, c), lambda i: (i, 0, 0, 0))
    shape = lambda c: jax.ShapeDtypeStruct((batches, levels, 2 * members, c), jnp.float32)
    return pl.pallas_call(
        gather_kernel,
        grid=(batches,),
        in_specs=[block(members, width)] * 2,
        out_specs=(block(2 * members, width), block(2 * members, BLK)),
        out_shape=(shape(width), shape(BLK)),
        cost_estimate=LONG,
    )(mine, got)


def one_hot(index, count):
    return (index[:, None] == jnp.arange(count, dtype=jnp.int32)[None, :]).astype(jnp.float32)


def pick(x, index):
    return lax.dynamic_index_in_dim(x, index, 0, keepdims=False)


def local(members, weights, taper_table, pair_blocks, pair_taper, pair_batch):
    member_loc, levels, column_count = members.shape
    ensemble = member_loc * lax.axis_size("member")
    regions = lax.axis_size("region")
    right = [(i, (i + 1) % regions) for i in range(regions)]
    left = [(j, i) for i, j in right]
    me = lax.axis_index("member")
    chip, core = me // 2, me % 2
    half = levels // 2

    states = jnp.transpose(members, (1, 0, 2))
    mine = lax.dynamic_slice_in_dim(states, core * half, half, 0)
    theirs = lax.dynamic_slice_in_dim(states, (1 - core) * half, half, 0)
    theirs, weights = lax.optimization_barrier((theirs, weights))
    states = jnp.concatenate([mine, lax.ppermute(theirs, "member", SWAP)], axis=1)

    near = chip ^ 1
    cross = CHIPS - 1 - chip
    one = jnp.where(core == 0, near, cross)
    two = jnp.where(core == 0, cross, near)
    both = CHIPS - 1 - near
    step_one, step_two = pairing(0), pairing(1)

    def to_owner(block):
        x = states[:, :, block * BLK : (block + 1) * BLK]
        got = lax.ppermute(jnp.stack([pick(x, one), pick(x, both)]), "member", step_one)
        last = lax.ppermute(jnp.stack([pick(x, two), got[1]]), "member", step_two)
        return pick(x, chip), got[0], last.reshape(-1, BLK)

    first, second = to_owner(0), to_owner(1)
    taken, pair_taper = lax.optimization_barrier((first[1], pair_taper))
    first = first[0], taken, first[2]
    tapers = jnp.dot(
        one_hot(pair_taper, taper_table.shape[0]), taper_table, precision=lax.Precision.HIGHEST
    ) / (ensemble - 1)
    targets = pair_blocks[:, 0]
    slot = targets * 6 + (pair_blocks[:, 1] - targets) * 2 + pair_batch
    coefs = jnp.sum(one_hot(slot, 12) * tapers[:, None], axis=0)
    rows = jnp.pad(coefs[None], ((0, 7), (0, BLK - 12)))
    w = jnp.transpose(weights, (0, 2, 1, 3))
    mine = lax.dynamic_slice_in_dim(w, core * half, half, 1)
    theirs = lax.dynamic_slice_in_dim(w, (1 - core) * half, half, 1)
    w, low = gathered(mine, lax.ppermute(theirs, "member", SWAP))
    rows, low = lax.optimization_barrier((rows, low))
    message = jnp.concatenate([*first, rows])
    after = lax.ppermute(message, "region", left)


    edge, own = covariances(message, *second, after)
    order = jnp.stack([chip, one, two, both])
    edge_near = lax.ppermute(edge, "member", step_one)
    own_near = lax.ppermute(own, "member", step_one)
    edge_far = lax.ppermute(jnp.stack([edge, edge_near]), "member", step_two)
    out, low = lax.optimization_barrier((jnp.stack([own, own_near]), low))
    own_far = lax.ppermute(out, "member", step_two)
    w_right = lax.ppermute(low, "region", left)
    edges = edge, edge_near, edge_far
    from_left = lax.ppermute(outward(order, after, w, edges), "region", right)
    kept, sent = increments(coefs, order, w, w_right, edges, (own, own_near, own_far))
    from_left = jnp.pad(from_left, ((0, 0), (0, 0), (0, column_count - BLK)))
    kept, sent = kept + from_left[:, :member_loc], sent + from_left[:, member_loc:]
    came = lax.ppermute(sent, "member", SWAP)
    change = jnp.where(
        core == 0, jnp.concatenate([kept, came]), jnp.concatenate([came, kept])
    )
    return members + jnp.transpose(change, (1, 0, 2))


def solution(mesh):
    placed = (
        P("member", None, "region"),
        P(None, "member", None, "region"),
        P(),
        P("region", None),
        P("region"),
        P("region"),
    )
    return jax.shard_map(
        local, mesh=mesh, in_specs=placed, out_specs=P("member", None, "region"), check_vma=False
    )
```

```python
import functools

import jax
import jax.numpy as jnp
from jax import lax
from jax.experimental import pallas as pl
from jax.experimental.pallas import tpu as pltpu
from jax.sharding import PartitionSpec as P

BLK = 128
CHIPS = 4
SWAP = [(i, i ^ 1) for i in range(2 * CHIPS)]
NEAR = [z ^ 1 for z in range(CHIPS)]
CROSS = [CHIPS - 1 - z for z in range(CHIPS)]


def pairing(step):
    moves = []
    for z in range(CHIPS):
        for core in range(2):
            partner = (NEAR if (core + step) % 2 == 0 else CROSS)[z]
            moves.append((2 * z + core, 2 * partner + core))
    return moves


def split(x):
    high = x.astype(jnp.bfloat16)
    return high, (x - high.astype(jnp.float32)).astype(jnp.bfloat16)


def product(a, b, dims):
    (ah, al), (bh, bl) = a, b
    dot = functools.partial(
        lax.dot_general, dimension_numbers=(dims, ((), ())), preferred_element_type=jnp.float32
    )
    return dot(ah, bh) + (dot(ah, bl) + dot(al, bh))


ROWS = ((0,), (0,))
PLAIN = ((1,), (0,))
LANES = ((1,), (1,))


def centred(*parts):
    count = sum(p.shape[0] for p in parts)
    mean = sum(jnp.sum(p, axis=0, keepdims=True) for p in parts) / count
    return split(jnp.concatenate([p - mean for p in parts], axis=0))


def first_kernel(message_ref, high_ref, low_ref, square_ref):
    first = centred(message_ref[: high_ref.shape[0]])
    high_ref[...], low_ref[...] = first
    square_ref[...] = product(first, first, ROWS)


def covariance_kernel(
    high_ref, low_ref, square_ref, kept_ref, got_ref, last_ref, message_ref, edge_ref, own_ref
):
    second = centred(kept_ref[...], got_ref[...], last_ref[...])
    first = high_ref[...], low_ref[...]
    d1 = product(second, second, ROWS)
    row = lax.broadcasted_iota(jnp.int32, (BLK, BLK), 0)
    col = lax.broadcasted_iota(jnp.int32, (BLK, BLK), 1)
    own_ref[:BLK] = jnp.where(row <= col, square_ref[...], d1)
    own_ref[BLK : 2 * BLK] = product(first, second, ROWS)
    diagonal = jnp.sum(jnp.where(row == col, d1, 0.0), axis=0, keepdims=True)
    own_ref[2 * BLK :] = jnp.broadcast_to(diagonal, (8, BLK))
    after = centred(message_ref[: high_ref.shape[0]])
    edge_ref[...] = product(second, after, ROWS)


LONG = pl.CostEstimate(flops=50_000_000_000, bytes_accessed=200_000_000, transcendentals=0)
TINY = pl.CostEstimate(flops=1000, bytes_accessed=1000, transcendentals=0)


def covariances(message, kept, got, last, after):
    ensemble = message.shape[0] - 8
    square = jax.ShapeDtypeStruct((BLK, BLK), jnp.float32)
    half = jax.ShapeDtypeStruct((ensemble, BLK), jnp.bfloat16)
    first = pl.pallas_call(first_kernel, out_shape=(half, half, square), cost_estimate=LONG)(message)
    return pl.pallas_call(
        covariance_kernel,
        out_shape=(square, jax.ShapeDtypeStruct((2 * BLK + 8, BLK), jnp.float32)),
        cost_estimate=TINY,
    )(*first, kept, got, last, after)


def pieces(own_ref, near_ref, far_ref):
    return own_ref[...], near_ref[...], far_ref[0], far_ref[1]


def outward_kernel(
    order_ref, message_ref, w_ref, own_ref, near_ref, far_ref, ahead_ref, out_ref
):
    for step, edge in enumerate(pieces(own_ref, near_ref, far_ref)):
        level = order_ref[step]
        mixed = message_ref[:1, :1] * w_ref[0, level] + message_ref[:1, 1:2] * w_ref[1, level]
        out_ref[level] = product(split(mixed), split(edge), PLAIN)


def outward(order, message, w, edges, ahead):
    levels, members = w.shape[1:3]
    whole = lambda x: pl.BlockSpec(x.shape, lambda i: (0,) * x.ndim)
    return pl.pallas_call(
        outward_kernel,
        grid=(1,),
        in_specs=[
            pl.BlockSpec(memory_space=pltpu.SMEM),
            pl.BlockSpec((8, BLK), lambda i: (message.shape[0] // 8 - 1, 0)),
            pl.BlockSpec((2, levels, members, BLK), lambda i: (0, 0, 0, 1)),
            *(whole(x) for x in edges),
            pl.BlockSpec(memory_space=pl.ANY),
        ],
        out_specs=pl.BlockSpec((levels, members, BLK), lambda i: (0, 0, 0)),
        out_shape=jax.ShapeDtypeStruct((levels, members, BLK), jnp.float32),
        cost_estimate=LONG,
    )(order, message, w, *edges, ahead)


def increment_kernel(
    coef_ref, order_ref, w_ref, wr_ref, e0_ref, e1_ref, e2_ref, c0_ref, c1_ref, c2_ref, kept_ref, sent_ref
):
    row = lax.broadcasted_iota(jnp.int32, (BLK, BLK), 0)
    col = lax.broadcasted_iota(jnp.int32, (BLK, BLK), 1)
    here, there = slice(0, BLK), slice(BLK, 2 * BLK)
    keep = kept_ref.shape[1]
    found = zip(pieces(e0_ref, e1_ref, e2_ref), pieces(c0_ref, c1_ref, c2_ref))
    for step, (edge, cov) in enumerate(found):
        level = order_ref[step]
        packed = cov[:BLK]
        upper = jnp.where(row <= col, packed, 0.0)
        strict = jnp.where(row < col, packed, 0.0)
        lower = jnp.where(row > col, packed, 0.0)
        diagonal = jnp.where(row == col, cov[2 * BLK : 2 * BLK + 1], 0.0)
        d0 = split(upper + strict.T)
        d1 = split(lower + lower.T + diagonal)
        c01 = split(cov[BLK : 2 * BLK])

        def mixed(ref, t, j, part=slice(None)):
            at = t * 6 + j * 2
            return split(
                coef_ref[at] * ref[0, level, :, part] + coef_ref[at + 1] * ref[1, level, :, part]
            )

        zero = product(mixed(w_ref, 0, 1, here), d0, PLAIN) + product(
            mixed(w_ref, 0, 2, there), c01, LANES
        )
        one = (
            product(mixed(w_ref, 1, 0, here), c01, PLAIN)
            + product(mixed(w_ref, 1, 1, there), d1, PLAIN)
            + product(mixed(wr_ref, 1, 2), split(edge), LANES)
        )
        for ref, rows in ((kept_ref, slice(0, keep)), (sent_ref, slice(keep, 2 * keep))):
            ref[level, :, here] = zero[rows]
            ref[level, :, there] = one[rows]


def increments(coefs, order, w, w_right, edges, covs):
    levels, members = w.shape[1:3]
    half = jax.ShapeDtypeStruct((levels, members // 2, 2 * BLK), jnp.float32)
    vmem, smem = (pl.BlockSpec(memory_space=m) for m in (pltpu.VMEM, pltpu.SMEM))
    return pl.pallas_call(
        increment_kernel,
        in_specs=[smem, smem] + [vmem] * 8,
        out_specs=(vmem, vmem),
        out_shape=(half, half),
        cost_estimate=TINY,
    )(coefs, order, w, w_right, *edges, *covs)


def gather_kernel(mine_ref, got_ref, w_ref, low_ref):
    keep = mine_ref.shape[2]
    for ref, rows in ((mine_ref, slice(0, keep)), (got_ref, slice(keep, 2 * keep))):
        w_ref[0, :, rows] = ref[0]
        low_ref[0, :, rows] = ref[0, :, :, :BLK]


def gathered(mine, got):
    batches, levels, members, width = mine.shape
    block = lambda m, c: pl.BlockSpec((1, levels, m, c), lambda i: (i, 0, 0, 0))
    shape = lambda c: jax.ShapeDtypeStruct((batches, levels, 2 * members, c), jnp.float32)
    return pl.pallas_call(
        gather_kernel,
        grid=(batches,),
        in_specs=[block(members, width)] * 2,
        out_specs=(block(2 * members, width), block(2 * members, BLK)),
        out_shape=(shape(width), shape(BLK)),
        cost_estimate=LONG,
    )(mine, got)


def one_hot(index, count):
    return (index[:, None] == jnp.arange(count, dtype=jnp.int32)[None, :]).astype(jnp.float32)


def pick(x, index):
    return lax.dynamic_index_in_dim(x, index, 0, keepdims=False)


def local(members, weights, taper_table, pair_blocks, pair_taper, pair_batch):
    member_loc, levels, column_count = members.shape
    ensemble = member_loc * lax.axis_size("member")
    regions = lax.axis_size("region")
    right = [(i, (i + 1) % regions) for i in range(regions)]
    left = [(j, i) for i, j in right]
    me = lax.axis_index("member")
    chip, core = me // 2, me % 2
    half = levels // 2

    states = jnp.transpose(members, (1, 0, 2))
    mine = lax.dynamic_slice_in_dim(states, core * half, half, 0)
    theirs = lax.dynamic_slice_in_dim(states, (1 - core) * half, half, 0)
    theirs, weights = lax.optimization_barrier((theirs, weights))
    states = jnp.concatenate([mine, lax.ppermute(theirs, "member", SWAP)], axis=1)

    near = chip ^ 1
    cross = CHIPS - 1 - chip
    one = jnp.where(core == 0, near, cross)
    two = jnp.where(core == 0, cross, near)
    both = CHIPS - 1 - near
    step_one, step_two = pairing(0), pairing(1)

    def to_owner(block):
        x = states[:, :, block * BLK : (block + 1) * BLK]
        got = lax.ppermute(jnp.stack([pick(x, one), pick(x, both)]), "member", step_one)
        last = lax.ppermute(jnp.stack([pick(x, two), got[1]]), "member", step_two)
        return pick(x, chip), got[0], last.reshape(-1, BLK)

    first, second = to_owner(0), to_owner(1)
    taken, pair_taper = lax.optimization_barrier((first[1], pair_taper))
    first = first[0], taken, first[2]
    tapers = jnp.dot(
        one_hot(pair_taper, taper_table.shape[0]), taper_table, precision=lax.Precision.HIGHEST
    ) / (ensemble - 1)
    targets = pair_blocks[:, 0]
    slot = targets * 6 + (pair_blocks[:, 1] - targets) * 2 + pair_batch
    coefs = jnp.sum(one_hot(slot, 12) * tapers[:, None], axis=0)
    rows = jnp.pad(coefs[None], ((0, 7), (0, BLK - 12)))
    w = jnp.transpose(weights, (0, 2, 1, 3))
    mine = lax.dynamic_slice_in_dim(w, core * half, half, 1)
    theirs = lax.dynamic_slice_in_dim(w, (1 - core) * half, half, 1)
    w, low = gathered(mine, lax.ppermute(theirs, "member", SWAP))
    rows, low = lax.optimization_barrier((rows, low))
    message = jnp.concatenate([*first, rows])
    after = lax.ppermute(message, "region", left)

    w_right = lax.ppermute(low, "region", left)

    edge, own = covariances(message, *second, after)
    order = jnp.stack([chip, one, two, both])
    edge_near = lax.ppermute(edge, "member", step_one)
    own_near = lax.ppermute(own, "member", step_one)
    edge_far = lax.ppermute(jnp.stack([edge, edge_near]), "member", step_two)
    own_far = lax.ppermute(jnp.stack([own, own_near]), "member", step_two)
    edges = edge, edge_near, edge_far
    from_left = lax.ppermute(outward(order, after, w, edges, w_right), "region", right)
    kept, sent = increments(coefs, order, w, w_right, edges, (own, own_near, own_far))
    from_left = jnp.pad(from_left, ((0, 0), (0, 0), (0, column_count - BLK)))
    kept, sent = kept + from_left[:, :member_loc], sent + from_left[:, member_loc:]
    came = lax.ppermute(sent, "member", SWAP)
    change = jnp.where(
        core == 0, jnp.concatenate([kept, came]), jnp.concatenate([came, kept])
    )
    return members + jnp.transpose(change, (1, 0, 2))


def solution(mesh):
    placed = (
        P("member", None, "region"),
        P(None, "member", None, "region"),
        P(),
        P("region", None),
        P("region"),
        P("region"),
    )
    return jax.shard_map(
        local, mesh=mesh, in_specs=placed, out_specs=P("member", None, "region"), check_vma=False
    )
```
